256 devices in a mesh: ctx: 32 (over y, x, core), tp: 8 (over z).
Axes of the slice: x: 4, y: 4, z: 8, core: 2. Of those that a mesh axis runs over, the one named last changes fastest.
Arguments:
- tokens: bfloat16 [32768, 2048], P(('ctx', 'tp')), may hold values from -6 to 6
- w_in: bfloat16 [2048, 8, 1288], P(None, 'tp'), may hold values from -0.125 to 0.125
- conv_weight: bfloat16 [4, 8, 768], P(None, 'tp'), may hold values from -3 to 3
- conv_bias: bfloat16 [8, 768], P('tp'), may hold values from -3 to 3
- dt_bias: float32 [64], P('tp'), may hold values from -3 to -1
- decay_rate: float32 [64], P('tp'), may hold values from 0 to 1, as said below
- skip_scale: float32 [64], P('tp'), may hold values from 0.5 to 1.5
- norm_gain: float32 [4096], P('tp'), may hold values from 0.1 to 1.9
- w_out: bfloat16 [4096, 2048], P('tp'), may hold values from -0.09375 to 0.09375
Outputs:
- mixed: bfloat16 [32768, 2048], P(('ctx', 'tp'))
The draws below stay inside these ranges and needn't reach their ends.
Inputs may be any that keep to these rules, and one draw needn't show every extreme that they name: `decay_rate`: positive per-head rates.
All inputs are finite; a program needn't handle non-finite values.
Results may differ from the reference program's by a relative error of at most 0.017.
Values may be sent and summed in bfloat16 or wider, within the bound.
No kernel may reach another device: no remote copies, remote signals or barrier semaphores. Data moves between devices by JAX's collectives and lax.ppermute only.
A program may use at most 128 MiB of HBM per device.

```python
import jax
import jax.numpy as jnp
from jax import lax

D = 2048
H = 64
P_SIZE = 64
N = 128
SPAN = 256
KCONV = 4
HEAD_DEV = 8
GRP_DEV = 1
XBC = 768
COLS = 1288
SEQ = 32768
N_TP = 8


def draw_decay_rate(key, part):
    key = jax.random.fold_in(key, 11)
    return jnp.exp(jax.random.uniform(key, (H,), jnp.float32, jnp.log(0.1 / SEQ), jnp.log(0.25)))


def block_levels(own_key, extent, cuts, least, top_value):
    level = 1.0
    for axis_at, shards_of in cuts:
        draws = jax.random.uniform(jax.random.fold_in(jax.random.fold_in(own_key, 6), axis_at), (shards_of,), jnp.float32, least / len(cuts), top_value / len(cuts))
        level = level * jnp.repeat(jnp.exp(draws), extent[axis_at] // shards_of).reshape((-1,) + (1,) * (len(extent) - 1 - axis_at))
    return level


def gaussian(rng, shape, width, bound, cuts=(), kind=jnp.bfloat16):
    loudness = block_levels(rng, shape, cuts, -0.22, 0.18) if cuts else 1.0
    entries = jax.random.normal(rng, shape, jnp.float32) * width * loudness
    return jnp.minimum(jnp.maximum(entries, -bound), bound).astype(kind)


def setup_inputs(seed: int = 0) -> dict:
    key_of = jax.random.split(jax.random.key(seed), 10)
    tokens = gaussian(key_of[0], (SEQ, D), 1.0, 6.0, ((0, 256),))
    w_in = gaussian(key_of[1], (D, N_TP, COLS), D ** -0.5, 0.125, ((1, 8),))
    conv_weight = gaussian(key_of[2], (KCONV, N_TP, XBC), KCONV ** -0.5, 3.0, ((1, 8),))
    conv_bias = gaussian(key_of[3], (N_TP, XBC), 0.5, 3.0, ((0, 8),))
    dt_bias = jnp.clip(-3.0 + 2.0 * jax.random.uniform(key_of[4], (H,), jnp.float32) ** block_levels(key_of[4], (H,), ((0, 8),), -0.2, 0.2), -3.0, -1.0)
    decay_rate = draw_decay_rate(jax.random.fold_in(key_of[9], 71), 0)
    skip_scale = jnp.clip(0.5 + 1.0 * jax.random.uniform(key_of[6], (H,), jnp.float32) ** block_levels(key_of[6], (H,), ((0, 8),), -0.2, 0.2), 0.5, 1.5)
    norm_gain = jnp.clip(1.0 + 0.18 * jax.random.normal(key_of[7], (H * P_SIZE,), jnp.float32), 0.1, 1.9)
    w_out = gaussian(key_of[8], (H * P_SIZE, D), (H * P_SIZE) ** -0.5, 0.09375, ((0, 8),))
    return {"tokens": tokens, "w_in": w_in, "conv_weight": conv_weight, "conv_bias": conv_bias, "dt_bias": dt_bias, "decay_rate": decay_rate, "skip_scale": skip_scale, "norm_gain": norm_gain, "w_out": w_out}


highest = lax.Precision.HIGHEST

def to_half(array):
    return lax.optimization_barrier(array.astype(jnp.bfloat16)).astype(jnp.float32)

def span_pass(state, pieces):
    span_x, span_b, span_c, span_dt, span_log = pieces
    per_group = state.shape[0] // span_b.shape[1]
    running = jnp.cumsum(span_log, axis=0)
    x_float = span_x.astype(jnp.float32)
    b_float = span_b.astype(jnp.float32)
    c_float = span_c.astype(jnp.float32)
    scores = jnp.einsum('tgn,sgn->gts', c_float, b_float, precision=highest)
    scores = jnp.repeat(scores, per_group, axis=0)
    length = span_log.shape[0]
    lower = jnp.arange(length)[:, None] >= jnp.arange(length)[None, :]
    spread = running.T[:, :, None] - running.T[:, None, :]
    decay = jnp.exp(jnp.where(lower[None], spread, -jnp.inf))
    weights = to_half(scores * decay * span_dt.T[:, None, :])
    inner = jnp.einsum('hts,shp->thp', weights, x_float, precision=highest)
    c_heads = jnp.repeat(c_float, per_group, axis=1)
    carried = jnp.einsum('thn,hpn->thp', c_heads, state, precision=highest) * jnp.exp(running)[:, :, None]
    final_log = running[-1]
    factor = jnp.exp(final_log[None, :] - running) * span_dt
    inflow = to_half(factor[:, :, None] * x_float)
    b_heads = jnp.repeat(b_float, per_group, axis=1)
    added = jnp.einsum('shp,shn->hpn', inflow, b_heads, precision=highest)
    new_state = state * jnp.exp(final_log)[:, None, None] + added
    return (new_state, inner + carried)

def run_spans(start_state, head_values, b_rows, c_rows, step_sizes, log_decay):
    number = head_values.shape[0] // SPAN

    def split(array):
        return array.reshape((number, SPAN) + array.shape[1:])
    final_state, outputs = lax.scan(span_pass, start_state, (split(head_values), split(b_rows), split(c_rows), split(step_sizes), split(log_decay)))
    return (final_state, outputs.reshape((number * SPAN,) + outputs.shape[2:]))

def prepare(projected, rim_rows, conv_w, conv_b, bias_dt, rates, width_h, xbc_width):
    row_count = projected.shape[0]
    gate_raw = projected[:, :width_h]
    xbc_raw = projected[:, width_h:width_h + xbc_width]
    dt_raw = projected[:, width_h + xbc_width:]
    padded = jnp.concatenate([rim_rows, xbc_raw], axis=0)
    taps = conv_w.shape[0]
    summed = jnp.zeros((row_count, xbc_width), jnp.float32) + conv_b.astype(jnp.float32)[None, :]
    for tap in range(taps):
        summed = summed + padded[tap:tap + row_count].astype(jnp.float32) * conv_w[tap].astype(jnp.float32)[None, :]
    xbc = jax.nn.silu(summed).astype(jnp.bfloat16)
    step_sizes = jax.nn.softplus(dt_raw.astype(jnp.float32) + bias_dt[None, :])
    log_decay = -rates[None, :] * step_sizes
    return (gate_raw, xbc, step_sizes, log_decay)

def split_xbc(xbc, width_h, groups_here):
    row_count = xbc.shape[0]
    group_cols = groups_here * N
    head_values = xbc[:, :width_h].reshape(row_count, width_h // P_SIZE, P_SIZE)
    b_rows = xbc[:, width_h:width_h + group_cols].reshape(row_count, groups_here, N)
    c_rows = xbc[:, width_h + group_cols:].reshape(row_count, groups_here, N)
    return (head_values, b_rows, c_rows)

def finish(outputs, head_values, gate_raw, skip_here, gain, groups_here):
    row_count = outputs.shape[0]
    whole = outputs + skip_here[None, :, None] * head_values.astype(jnp.float32)
    gated = whole.reshape(row_count, -1) * jax.nn.silu(gate_raw.astype(jnp.float32))
    grouped = gated.reshape(row_count, groups_here, -1)
    factor = lax.rsqrt(lax.optimization_barrier(jnp.mean(grouped * grouped, axis=2, keepdims=True)) + 1e-05)
    normed = (grouped * factor).reshape(row_count, -1) * gain[None, :]
    return normed.astype(jnp.bfloat16)

def reference(tokens, w_in, conv_weight, conv_bias, dt_bias, decay_rate, skip_scale, norm_gain, w_out):
    width_h = HEAD_DEV * P_SIZE

    def one_shard(total, pieces):
        weights, conv_w, conv_b, bias_dt, rates, skip_here, gain, w_down = pieces
        projected = jnp.dot(tokens, weights, preferred_element_type=jnp.float32).astype(jnp.bfloat16)
        rim_rows = jnp.zeros((KCONV - 1, XBC), jnp.bfloat16)
        gate_raw, xbc, step_sizes, log_decay = prepare(projected, rim_rows, conv_w, conv_b, bias_dt, rates, width_h, XBC)
        head_values, b_rows, c_rows = split_xbc(xbc, width_h, GRP_DEV)
        start_state = jnp.zeros((HEAD_DEV, P_SIZE, N), jnp.float32)
        final_state, outputs = run_spans(start_state, head_values, b_rows, c_rows, step_sizes, log_decay)
        hidden = finish(outputs, head_values, gate_raw, skip_here, gain, GRP_DEV)
        partial_out = jnp.dot(hidden, w_down, preferred_element_type=jnp.float32).astype(jnp.bfloat16)
        partial_out = lax.optimization_barrier(partial_out).astype(jnp.float32)
        return (total + partial_out, None)
    stacked = (jnp.transpose(w_in, (1, 0, 2)), jnp.transpose(conv_weight, (1, 0, 2)), conv_bias, dt_bias.reshape(N_TP, HEAD_DEV), decay_rate.reshape(N_TP, HEAD_DEV), skip_scale.reshape(N_TP, HEAD_DEV), norm_gain.reshape(N_TP, width_h), w_out.reshape(N_TP, width_h, D))
    total, unused = lax.scan(one_shard, jnp.zeros((SEQ, D), jnp.float32), stacked)
    return total.astype(jnp.bfloat16)
```

```python
import functools
import math

import jax
import jax.numpy as jnp
from jax import lax
from jax.experimental import pallas as pl
from jax.experimental.pallas import tpu as pltpu
from jax.sharding import PartitionSpec as P

P_SIZE = 64
N = 128
CHUNK = 128
LOG2E = math.log2(math.e)
VMEM_LIMIT = 48 * 1024 * 1024

SLOT_OF_DISTANCE = (6, 0, 2, 4, 7, 5, 3, 1)
FIRST_SENT = (4, 3, -3)
LATER_SENT = (2, -2, 1, -1, 0)


def turned(value, axis, steps):
    count = lax.axis_size(axis)
    return lax.ppermute(value, axis, [(i, (i + steps) % count) for i in range(count)])


def next_block(value):
    count = lax.axis_size("ctx")
    return lax.ppermute(value, "ctx", [(i, i + 1) for i in range(count - 1)])


def rows_of_heads(per_head, heads):
    width = per_head.shape[1]
    return jnp.concatenate(
        [jnp.broadcast_to(per_head[h : h + 1], (P_SIZE, width)) for h in range(heads)], axis=0
    )


def project_kernel(count, *refs):
    pieces = refs[:count]
    w_ref = refs[count]
    out_ref, rows_ref = refs[-2:]

    @pl.when(pl.program_id(0) == 0)
    def _():
        at = 0
        for piece in pieces:
            size = piece.shape[0]
            rows_ref[at : at + size, :] = piece[...]
            at += size

    out_ref[...] = lax.dot_general(
        w_ref[...], rows_ref[...], (((1,), (1,)), ((), ())), preferred_element_type=jnp.float32
    ).astype(jnp.bfloat16)


def project(pieces, w_t, whole, row_count, block_at):
    cols, depth = w_t.shape
    rows = sum(piece.shape[0] for piece in pieces)
    tile = 432
    grid = (pl.cdiv(cols, tile),)
    in_specs = [pl.BlockSpec(piece.shape, lambda i: (0, 0)) for piece in pieces]
    in_specs.append(pl.BlockSpec((tile, depth), lambda i: (i, 0)))
    operands = list(pieces) + [w_t]
    aliases = {}
    if whole is not None:
        in_specs.append(pl.BlockSpec(memory_space=pl.ANY))
        operands.append(whole)
        aliases = {len(operands) - 1: 0}
    return pl.pallas_call(
        functools.partial(project_kernel, len(pieces)),
        grid=grid,
        in_specs=in_specs,
        out_specs=pl.BlockSpec((tile, rows), lambda i: (i, block_at)),
        out_shape=jax.ShapeDtypeStruct((cols, row_count), jnp.bfloat16),
        scratch_shapes=[pltpu.VMEM((rows, depth), jnp.bfloat16)],
        input_output_aliases=aliases,
        compiler_params=pltpu.CompilerParams(vmem_limit_bytes=VMEM_LIMIT),
        cost_estimate=pl.CostEstimate(
            flops=2 * rows * cols * depth,
            bytes_accessed=2 * (cols * depth + rows * depth + rows * cols),
            transcendentals=0,
        ),
        name="project",
    )(*operands)


def states_kernel(
    heads,
    perm_ref,
    proj_ref,
    halo_ref,
    taps_ref,
    bias_ref,
    head_ref,
    xbc_ref,
    run_ref,
    col_ref,
    cum_ref,
    local_ref,
    payload_ref,
    tail_ref,
    state_ref,
    total_ref,
):
    width = heads * P_SIZE
    step = pl.program_id(0)

    @pl.when(step == 0)
    def _():
        tail_ref[...] = halo_ref[...].astype(jnp.float32)
        state_ref[...] = jnp.zeros_like(state_ref)
        total_ref[...] = jnp.zeros_like(total_ref)

    lanes = lax.broadcasted_iota(jnp.int32, (P_SIZE, CHUNK), 1)
    xbc_width = xbc_ref.shape[0]
    for at in range(0, xbc_width, P_SIZE):
        raw = proj_ref[width + at : width + at + P_SIZE, :].astype(jnp.float32)
        tail = tail_ref[at : at + P_SIZE, :]
        acc = bias_ref[at : at + P_SIZE, :] + raw * taps_ref[3, at : at + P_SIZE, :]
        for back in (1, 2, 3):
            moved = jnp.where(
                lanes < back, pltpu.roll(tail, back, 1), pltpu.roll(raw, back, 1)
            )
            acc = acc + moved * taps_ref[3 - back, at : at + P_SIZE, :]
        tail_ref[at : at + P_SIZE, :] = raw
        xbc_ref[at : at + P_SIZE, :] = (acc * (0.5 * jnp.tanh(0.5 * acc) + 0.5)).astype(
            jnp.bfloat16
        )

    dt_raw = proj_ref[width + xbc_width : width + xbc_width + heads, :].astype(jnp.float32)
    shifted = dt_raw + head_ref[0]
    dt = jnp.maximum(shifted, 0.0) + jnp.log1p(jnp.exp(-jnp.abs(shifted)))
    run = -head_ref[1] * dt
    lane8 = lax.broadcasted_iota(jnp.int32, (heads, CHUNK), 1)
    reach = 1
    while reach < CHUNK:
        run = run + jnp.where(lane8 >= reach, pltpu.roll(run, reach, 1), 0.0)
        reach *= 2
    total = jnp.broadcast_to(run[:, CHUNK - 1 :], (heads, CHUNK))
    run_ref[...] = run
    col_ref[...] = run * LOG2E - jnp.log2(dt)
    cum_ref[...] = total_ref[...]
    factor = jnp.exp(total - run) * dt
    keep = jnp.exp(total)
    b_t = xbc_ref[width : width + N, :]
    inflow = (xbc_ref[:width, :].astype(jnp.float32) * rows_of_heads(factor, heads)).astype(
        jnp.bfloat16
    )
    added = lax.dot_general(
        inflow, b_t, (((1,), (1,)), ((), ())), preferred_element_type=jnp.float32
    )
    before = state_ref[...]
    local_ref[0] = before
    after = before * rows_of_heads(keep, heads) + added
    state_ref[...] = after
    all_total = total_ref[...] + total
    total_ref[...] = all_total

    @pl.when(step == pl.num_programs(0) - 1)
    def _():
        row = lax.broadcasted_iota(jnp.int32, (16, N), 0)
        high = all_total.astype(jnp.bfloat16).astype(jnp.float32)
        mid = (all_total - high).astype(jnp.bfloat16).astype(jnp.float32)
        low = all_total - high - mid
        pieces = width // 16
        for piece in range(pieces):
            h = piece * 16 // P_SIZE
            payload_ref[piece, :16, :] = after[piece * 16 : piece * 16 + 16].astype(jnp.bfloat16)
            parts = jnp.where(
                row == 0,
                jnp.broadcast_to(high[h : h + 1], (16, N)),
                jnp.where(
                    row == 1,
                    jnp.broadcast_to(mid[h : h + 1], (16, N)),
                    jnp.broadcast_to(low[h : h + 1], (16, N)),
                ),
            )
            payload_ref[piece, 16:, :] = parts.astype(jnp.bfloat16)


def chunk_states(perm, projected, halo, taps, bias, head_values):
    heads = head_values.shape[1]
    width = heads * P_SIZE
    cols, rows = projected.shape
    xbc_width = taps.shape[1]
    chunks = rows // CHUNK
    pieces = width // 16
    column = lambda j, perm: (0, j)
    return pl.pallas_call(
        functools.partial(states_kernel, heads),
        grid_spec=pltpu.PrefetchScalarGridSpec(
            num_scalar_prefetch=1,
            grid=(chunks,),
            in_specs=[
                pl.BlockSpec((cols, CHUNK), lambda j, perm: (0, perm[j])),
                pl.BlockSpec(halo.shape, lambda j, perm: (0, 0)),
                pl.BlockSpec(taps.shape, lambda j, perm: (0, 0, 0)),
                pl.BlockSpec(bias.shape, lambda j, perm: (0, 0)),
                pl.BlockSpec(head_values.shape, lambda j, perm: (0, 0, 0)),
            ],
            out_specs=[
                pl.BlockSpec((xbc_width, CHUNK), column),
                pl.BlockSpec((heads, CHUNK), column),
                pl.BlockSpec((heads, CHUNK), column),
                pl.BlockSpec((heads, CHUNK), column),
                pl.BlockSpec((1, width, N), lambda j, perm: (j, 0, 0)),
                pl.BlockSpec((pieces, 32, N), lambda j, perm: (0, 0, 0)),
            ],
            scratch_shapes=[
                pltpu.VMEM((xbc_width, CHUNK), jnp.float32),
                pltpu.VMEM((width, N), jnp.float32),
                pltpu.VMEM((heads, CHUNK), jnp.float32),
            ],
        ),
        out_shape=[
            jax.ShapeDtypeStruct((xbc_width, rows), jnp.bfloat16),
            jax.ShapeDtypeStruct((heads, rows), jnp.float32),
            jax.ShapeDtypeStruct((heads, rows), jnp.float32),
            jax.ShapeDtypeStruct((heads, rows), jnp.float32),
            jax.ShapeDtypeStruct((chunks, width, N), jnp.float32),
            jax.ShapeDtypeStruct((pieces, 32, N), jnp.bfloat16),
        ],
        compiler_params=pltpu.CompilerParams(vmem_limit_bytes=VMEM_LIMIT),
        cost_estimate=pl.CostEstimate(
            flops=2 * rows * width * N + 30 * rows * xbc_width,
            bytes_accessed=8 * 1024 * 1024,
            transcendentals=2 * rows * xbc_width,
        ),
        name="chunk_states",
    )(perm, projected, halo, taps, bias, head_values)


def inner_kernel(heads, perm_ref, gate_ref, xbc_ref, run_ref, col_ref, skip_ref, own_ref, open_ref):
    width = heads * P_SIZE
    b_t = xbc_ref[width : width + N, :]
    c_t = xbc_ref[width + N : width + 2 * N, :]
    scores = lax.dot_general(
        b_t, c_t, (((0,), (0,)), ((), ())), preferred_element_type=jnp.float32
    )
    sender = lax.broadcasted_iota(jnp.int32, (CHUNK, CHUNK), 0)
    taker = lax.broadcasted_iota(jnp.int32, (CHUNK, CHUNK), 1)
    lower = sender <= taker
    run = run_ref[...] * LOG2E
    columns = jnp.transpose(col_ref[...])
    for h in range(heads):
        top = h * P_SIZE
        spread = run[h : h + 1, :] - columns[:, h : h + 1]
        weights = jnp.where(lower, scores * jnp.exp2(spread), 0.0).astype(jnp.bfloat16)
        x_t = xbc_ref[top : top + P_SIZE, :]
        own = jnp.dot(x_t, weights, preferred_element_type=jnp.float32)
        own_ref[top : top + P_SIZE, :] = (
            own + skip_ref[top : top + P_SIZE, :] * x_t.astype(jnp.float32)
        )
        gate = gate_ref[top : top + P_SIZE, :].astype(jnp.float32)
        open_ref[top : top + P_SIZE, :] = gate * (0.5 * jnp.tanh(0.5 * gate) + 0.5)


def inner(perm, projected, xbc, run, col, skip):
    width = skip.shape[0]
    heads = width // P_SIZE
    rows = xbc.shape[1]
    chunks = rows // CHUNK
    column = lambda j, perm: (0, j)
    return pl.pallas_call(
        functools.partial(inner_kernel, heads),
        grid_spec=pltpu.PrefetchScalarGridSpec(
            num_scalar_prefetch=1,
            grid=(chunks,),
            in_specs=[
                pl.BlockSpec((width, CHUNK), lambda j, perm: (0, perm[j])),
                pl.BlockSpec((xbc.shape[0], CHUNK), column),
                pl.BlockSpec((heads, CHUNK), column),
                pl.BlockSpec((heads, CHUNK), column),
                pl.BlockSpec((width, CHUNK), lambda j, perm: (0, 0)),
            ],
            out_specs=[
                pl.BlockSpec((width, CHUNK), column),
                pl.BlockSpec((width, CHUNK), column),
            ],
        ),
        out_shape=[
            jax.ShapeDtypeStruct((width, rows), jnp.float32),
            jax.ShapeDtypeStruct((width, rows), jnp.float32),
        ],
        compiler_params=pltpu.CompilerParams(vmem_limit_bytes=VMEM_LIMIT),
        cost_estimate=pl.CostEstimate(
            flops=2 * rows * CHUNK * (width + N) + 8 * rows * CHUNK * heads,
            bytes_accessed=8 * 1024 * 1024,
            transcendentals=rows * (CHUNK * heads + width),
        ),
        name="inner",
    )(perm, projected, xbc, run, col, skip)


def prefix_kernel(got_ref, out_ref):
    count = got_ref.shape[0]
    state = jnp.zeros((16, N), jnp.float32)
    for c in range(count):
        out_ref[c] = state.astype(jnp.bfloat16)
        if c < count - 1:
            tail = got_ref[c, 16:, :].astype(jnp.float32)
            log_decay = tail[0:1] + tail[1:2] + tail[2:3]
            state = state * jnp.exp(log_decay) + got_ref[c, :16, :].astype(jnp.float32)


def prefix(got):
    count = got.shape[0]
    return pl.pallas_call(
        prefix_kernel,
        out_shape=jax.ShapeDtypeStruct((count, 16, N), jnp.bfloat16),
        name="prefix",
    )(got)


def finish_kernel(
    heads,
    order_ref,
    own_ref,
    open_ref,
    c_ref,
    run_ref,
    cum_ref,
    local_ref,
    state_ref,
    gain_ref,
    w_ref,
    out_ref,
    u_ref,
):
    width = heads * P_SIZE
    keep = jnp.exp(cum_ref[...])
    start = (
        local_ref[0] + state_ref[...].astype(jnp.float32) * rows_of_heads(keep, heads)
    ).astype(jnp.bfloat16)
    carried = jnp.dot(start, c_ref[...], preferred_element_type=jnp.float32)
    grown = jnp.exp(run_ref[...])
    squares = jnp.zeros((1, CHUNK), jnp.float32)
    for h in range(heads):
        part = slice(h * P_SIZE, (h + 1) * P_SIZE)
        u = (own_ref[part, :] + carried[part, :] * grown[h : h + 1, :]) * open_ref[part, :]
        squares = squares + jnp.sum(u * u, axis=0, keepdims=True)
        u_ref[part, :] = u
    scale = lax.rsqrt(squares * (1.0 / width) + 1e-05)
    hidden = (u_ref[...] * scale * gain_ref[...]).astype(jnp.bfloat16)
    out_ref[0] = lax.dot_general(
        hidden, w_ref[...], (((0,), (0,)), ((), ())), preferred_element_type=jnp.float32
    ).astype(jnp.bfloat16)


def finish(order, own, opened, xbc, run, cum, local, state, gain, w_out):
    width, rows = own.shape
    heads = width // P_SIZE
    count = order.shape[0]
    out_width = w_out.shape[1]
    column = lambda j, order: (0, order[j])
    fixed = lambda j, order: (0, 0)
    c_block = (width + N) // N
    return pl.pallas_call(
        functools.partial(finish_kernel, heads),
        grid_spec=pltpu.PrefetchScalarGridSpec(
            num_scalar_prefetch=1,
            grid=(count,),
            in_specs=[
                pl.BlockSpec((width, CHUNK), column),
                pl.BlockSpec((width, CHUNK), column),
                pl.BlockSpec((N, CHUNK), lambda j, order: (c_block, order[j])),
                pl.BlockSpec((heads, CHUNK), column),
                pl.BlockSpec((heads, CHUNK), column),
                pl.BlockSpec((1, width, N), lambda j, order: (order[j], 0, 0)),
                pl.BlockSpec((width, N), fixed),
                pl.BlockSpec((width, CHUNK), fixed),
                pl.BlockSpec((width, out_width), fixed),
            ],
            out_specs=pl.BlockSpec((1, CHUNK, out_width), lambda j, order: (j, 0, 0)),
            scratch_shapes=[pltpu.VMEM((width, CHUNK), jnp.float32)],
        ),
        out_shape=jax.ShapeDtypeStruct((count, CHUNK, out_width), jnp.bfloat16),
        compiler_params=pltpu.CompilerParams(vmem_limit_bytes=VMEM_LIMIT),
        cost_estimate=pl.CostEstimate(
            flops=2 * count * CHUNK * width * (out_width + N),
            bytes_accessed=2 * width * out_width + count * 1024 * 1024,
            transcendentals=0,
        ),
        name="finish",
    )(order, own, opened, xbc, run, cum, local, state, gain, w_out)


def per_device(
    tokens, w_in, conv_weight, conv_bias, dt_bias, decay_rate, skip_scale, norm_gain, w_out
):
    me = lax.axis_index("tp")
    n_tp = lax.axis_size("tp")
    width = norm_gain.shape[0]
    heads = decay_rate.shape[0]
    rows = tokens.shape[0] * n_tp
    half = tokens.shape[0] // 2
    w_t = jnp.transpose(w_in.reshape(w_in.shape[0], w_in.shape[2]))
    xbc_width = conv_weight.shape[2]

    edge = lax.all_gather(next_block(tokens[-8:]), "tp", axis=0)[n_tp - 1]
    halo = lax.dot_general(
        w_t[width : width + xbc_width], edge, (((1,), (1,)), ((), ())),
        preferred_element_type=jnp.float32,
    ).astype(jnp.bfloat16)
    halo = jnp.pad(halo, ((0, 0), (CHUNK - 8, 0)))

    taps = jnp.broadcast_to(
        conv_weight.reshape(conv_weight.shape[0], xbc_width, 1).astype(jnp.float32),
        (conv_weight.shape[0], xbc_width, CHUNK),
    )
    bias = jnp.broadcast_to(
        conv_bias.reshape(xbc_width, 1).astype(jnp.float32), (xbc_width, CHUNK)
    )
    head_values = jnp.broadcast_to(
        jnp.stack([dt_bias, decay_rate])[:, :, None], (2, heads, CHUNK)
    )
    skip = jnp.broadcast_to(jnp.repeat(skip_scale, P_SIZE)[:, None], (width, CHUNK))
    gain = jnp.broadcast_to(norm_gain[:, None], (width, CHUNK))
    perm = jnp.asarray(SLOT_OF_DISTANCE, jnp.int32)[(jnp.arange(n_tp) - me) % n_tp]

    right = [tokens[:half], tokens[half:]]
    left = [tokens[:half], tokens[half:]]
    projected = project([tokens], w_t, None, rows, 6)
    for hop in range(1, 4):
        right = [turned(right[0], "tp", 1), turned(right[1], "tp", 1)]
        left = [turned(left[0], "tp", -1), turned(left[1], "tp", -1)]
        projected = project(left + right, w_t, projected, rows, hop - 1)
    last = [turned(right[0], "tp", 1), turned(left[1], "tp", -1)]
    projected = project(last, w_t, projected, rows, 7)

    xbc, run, col, cum, local, payload = chunk_states(
        perm, projected, halo, taps, bias, head_values
    )
    got = lax.all_to_all(payload, "ctx", 0, 0, tiled=True)
    own, opened = inner(perm, projected, xbc, run, col, skip)
    state = lax.all_to_all(prefix(got), "ctx", 0, 0, tiled=True).reshape(width, N)

    def finished(distances):
        order = ((me + jnp.asarray(distances, jnp.int32)) % n_tp).astype(jnp.int32)
        return finish(order, own, opened, xbc, run, cum, local, state, gain, w_out)

    first, later = finished(FIRST_SENT), finished(LATER_SENT)
    blocks = {d: first[i] for i, d in enumerate(FIRST_SENT)}
    blocks.update({d: later[i] for i, d in enumerate(LATER_SENT)})

    def block(distance, part):
        return blocks[distance][part * half : (part + 1) * half]

    def plus(moving, distance, part):
        return (
            moving.astype(jnp.float32) + block(distance, part).astype(jnp.float32)
        ).astype(jnp.bfloat16)

    r0, l1 = turned(block(4, 0), "tp", 1), turned(block(4, 1), "tp", -1)
    r1, l0 = turned(block(3, 1), "tp", 1), turned(block(-3, 0), "tp", -1)
    for k in (3, 2, 1):
        r0 = turned(plus(r0, k, 0), "tp", 1)
        l1 = turned(plus(l1, -k, 1), "tp", -1)
        if k > 1:
            r1 = turned(plus(r1, k - 1, 1), "tp", 1)
            l0 = turned(plus(l0, 1 - k, 0), "tp", -1)
    top = r0.astype(jnp.float32) + l0.astype(jnp.float32) + block(0, 0).astype(jnp.float32)
    bottom = r1.astype(jnp.float32) + l1.astype(jnp.float32) + block(0, 1).astype(jnp.float32)
    return jnp.concatenate([top, bottom], axis=0).astype(jnp.bfloat16)


def solution(mesh):
    placed = (
        P(("ctx", "tp"), None),
        P(None, "tp", None),
        P(None, "tp", None),
        P("tp", None),
        P("tp"),
        P("tp"),
        P("tp"),
        P("tp"),
        P("tp", None),
    )
    return jax.shard_map(
        per_device, mesh=mesh, in_specs=placed, out_specs=P(("ctx", "tp"), None), check_vma=False
    )
```

```python
import functools
import math

import jax
import jax.numpy as jnp
from jax import lax
from jax.experimental import pallas as pl
from jax.experimental.pallas import tpu as pltpu
from jax.sharding import PartitionSpec as P

P_SIZE = 64
N = 128
CHUNK = 128
LOG2E = math.log2(math.e)
VMEM_LIMIT = 36 * 1024 * 1024

PLACE_OF_DISTANCE = ((3, 0), (0, 0), (1, 0), (2, 0), (3, 1), (2, 1), (1, 1), (0, 1))
ARRAYS = 4
FIRST_SENT = (4, 3, -3)
LATER_SENT = (2, -2, 1, -1, 0)


def turned(value, axis, steps):
    count = lax.axis_size(axis)
    return lax.ppermute(value, axis, [(i, (i + steps) % count) for i in range(count)])


def next_block(value):
    count = lax.axis_size("ctx")
    return lax.ppermute(value, "ctx", [(i, i + 1) for i in range(count - 1)])


def rows_of_heads(per_head, heads):
    width = per_head.shape[1]
    return jnp.concatenate(
        [jnp.broadcast_to(per_head[h : h + 1], (P_SIZE, width)) for h in range(heads)], axis=0
    )


def project(pieces, w_t):
    rows = jnp.concatenate(pieces, axis=0) if len(pieces) > 1 else pieces[0]
    return lax.dot_general(
        w_t, rows, (((1,), (1,)), ((), ())), preferred_element_type=jnp.float32
    ).astype(jnp.bfloat16)


def chunk_of(arrays, distance):
    which, side = PLACE_OF_DISTANCE[distance]
    return arrays[which].at[:, side * CHUNK : (side + 1) * CHUNK]


def whole(*shapes):
    def zeros(rank):
        return lambda i: (0,) * rank

    return [pl.BlockSpec(tuple(item.shape), zeros(len(item.shape))) for item in shapes]


def convolve(raw, before, taps_ref, bias_ref, at):
    part = pl.ds(at, P_SIZE)
    lanes = lax.broadcasted_iota(jnp.int32, raw.shape, 1)
    acc = bias_ref[part, :] + raw * taps_ref[3, part, :]
    for back in (1, 2, 3):
        moved = jnp.where(lanes < back, pltpu.roll(before, back, 1), pltpu.roll(raw, back, 1))
        acc = acc + moved * taps_ref[3 - back, part, :]
    return (acc * (0.5 * jnp.tanh(0.5 * acc) + 0.5)).astype(jnp.bfloat16)


def added_state(xbc, factor, heads):
    width = heads * P_SIZE
    inflow = (xbc[:width].astype(jnp.float32) * rows_of_heads(factor, heads)).astype(jnp.bfloat16)
    return lax.dot_general(
        inflow,
        xbc[width : width + N],
        (((1,), (1,)), ((), ())),
        preferred_element_type=jnp.float32,
    )


def states_kernel(heads, chunks, me_ref, *refs):
    arrays = refs[:ARRAYS]
    halo_ref, taps_ref, bias_ref, head_ref = refs[ARRAYS : ARRAYS + 4]
    xbc_ref, run_ref, col_ref, cum_ref, local_ref, payload_ref = refs[ARRAYS + 4 : ARRAYS + 10]
    raw_ref, dt_ref = refs[ARRAYS + 10 :]
    width = heads * P_SIZE
    xbc_width = xbc_ref.shape[1]
    me = me_ref[0]
    raw_ref[0] = halo_ref[...]
    for distance in range(chunks):
        j = lax.rem(me + distance, chunks)
        source = chunk_of(arrays, distance)
        raw_ref[j + 1] = source[width : width + xbc_width, :]
        dt_ref[j] = source[width + xbc_width : width + xbc_width + heads, :].astype(jnp.float32)

    shifted = dt_ref[...] + head_ref[0]
    dt = jnp.maximum(shifted, 0.0) + jnp.log1p(jnp.exp(-jnp.abs(shifted)))
    run = (-head_ref[1] * dt).reshape(chunks * heads, CHUNK)
    lanes = lax.broadcasted_iota(jnp.int32, run.shape, 1)
    reach = 1
    while reach < CHUNK:
        run = run + jnp.where(lanes >= reach, pltpu.roll(run, reach, 1), 0.0)
        reach *= 2
    run = run.reshape(chunks, heads, CHUNK)
    total = jnp.broadcast_to(run[:, :, CHUNK - 1 :], run.shape)
    run_ref[...] = run
    col_ref[...] = run * LOG2E - jnp.log2(dt)
    factor = jnp.exp(total - run) * dt
    keep = jnp.exp(total)

    cum = jnp.zeros((heads, CHUNK), jnp.float32)
    state = jnp.zeros((width, N), jnp.float32)
    for j in range(chunks):
        for at in range(0, xbc_width, P_SIZE):
            part = pl.ds(at, P_SIZE)
            xbc_ref[j, part, :] = convolve(
                raw_ref[j + 1, part, :].astype(jnp.float32),
                raw_ref[j, part, :].astype(jnp.float32),
                taps_ref,
                bias_ref,
                at,
            )
        cum_ref[j] = cum
        local_ref[j] = state
        added = added_state(xbc_ref[j], factor[j], heads)
        state = state * rows_of_heads(keep[j], heads) + added if j else added
        cum = cum + total[j]

    row = lax.broadcasted_iota(jnp.int32, (16, N), 0)
    all_keep = jnp.exp(cum)
    high = all_keep.astype(jnp.bfloat16).astype(jnp.float32)
    mid = (all_keep - high).astype(jnp.bfloat16).astype(jnp.float32)
    low = all_keep - high - mid
    for piece in range(width // 16):
        h = piece * 16 // P_SIZE
        payload_ref[piece, :16, :] = state[piece * 16 : piece * 16 + 16].astype(jnp.bfloat16)
        parts = jnp.where(
            row == 0,
            jnp.broadcast_to(high[h : h + 1], (16, N)),
            jnp.where(
                row == 1,
                jnp.broadcast_to(mid[h : h + 1], (16, N)),
                jnp.broadcast_to(low[h : h + 1], (16, N)),
            ),
        )
        payload_ref[piece, 16:, :] = parts.astype(jnp.bfloat16)


def chunk_states(me, arrays, halo, taps, bias, head_values):
    heads = head_values.shape[1]
    width = heads * P_SIZE
    xbc_width = taps.shape[1]
    rows = sum(array.shape[1] for array in arrays)
    chunks = rows // CHUNK
    operands = [*arrays, halo, taps, bias, head_values]
    small = jax.ShapeDtypeStruct((chunks, heads, CHUNK), jnp.float32)
    results = [
        jax.ShapeDtypeStruct((chunks, xbc_width, CHUNK), jnp.bfloat16),
        small,
        small,
        small,
        jax.ShapeDtypeStruct((chunks, width, N), jnp.float32),
        jax.ShapeDtypeStruct((width // 16, 32, N), jnp.bfloat16),
    ]
    return pl.pallas_call(
        functools.partial(states_kernel, heads, chunks),
        grid=(1,),
        in_specs=[pl.BlockSpec(memory_space=pltpu.SMEM)] + whole(*operands),
        out_specs=whole(*results),
        out_shape=results,
        scratch_shapes=[
            pltpu.VMEM((chunks + 1, xbc_width, CHUNK), jnp.bfloat16),
            pltpu.VMEM((chunks, heads, CHUNK), jnp.float32),
        ],
        compiler_params=pltpu.CompilerParams(vmem_limit_bytes=VMEM_LIMIT),
        cost_estimate=pl.CostEstimate(
            flops=2 * rows * width * N + 30 * rows * xbc_width,
            bytes_accessed=8 * 1024 * 1024,
            transcendentals=2 * rows * xbc_width,
        ),
        name="chunk_states",
    )(me, *operands)


def prefix_kernel(got_ref, out_ref):
    count = got_ref.shape[0]
    tails = [got_ref[c, 16:, :].astype(jnp.float32) for c in range(count - 1)]
    keeps = [jnp.broadcast_to(tail[0:1] + tail[1:2] + tail[2:3], (16, N)) for tail in tails]
    state = jnp.zeros((16, N), jnp.float32)
    for c in range(count):
        out_ref[c] = state.astype(jnp.bfloat16)
        if c < count - 1:
            state = state * keeps[c] + got_ref[c, :16, :].astype(jnp.float32)


def prefix(got):
    count = got.shape[0]
    return pl.pallas_call(
        prefix_kernel,
        out_shape=jax.ShapeDtypeStruct((count, 16, N), jnp.bfloat16),
        compiler_params=pltpu.CompilerParams(vmem_limit_bytes=4 * 1024 * 1024),
        name="prefix",
    )(got)


def finish_kernel(heads, group, halves, me_ref, skip_ref, *refs):
    arrays = refs[:ARRAYS]
    xbc_ref, run_ref, col_ref, cum_ref, local_ref = refs[ARRAYS : ARRAYS + 5]
    state_ref, gain_ref, w_ref = refs[ARRAYS + 5 : ARRAYS + 8]
    outs = refs[ARRAYS + 8 : -2]
    hidden_ref, u_ref = refs[-2:]
    width = heads * P_SIZE
    count = len(PLACE_OF_DISTANCE)
    sender = lax.broadcasted_iota(jnp.int32, (CHUNK, CHUNK), 0)
    taker = lax.broadcasted_iota(jnp.int32, (CHUNK, CHUNK), 1)
    lower = sender <= taker
    before = state_ref[...].astype(jnp.float32)
    gains = jnp.transpose(gain_ref[...])
    gain = jnp.concatenate(
        [jnp.broadcast_to(gains[:, k : k + 1], (N, CHUNK)) for k in range(width // N)], axis=0
    )
    for place, distance in enumerate(group):
        j = lax.rem(me_ref[0] + distance + count, count)
        gate_ref = chunk_of(arrays, distance % count)
        b_t = xbc_ref[j, width : width + N, :]
        c_t = xbc_ref[j, width + N : width + 2 * N, :]
        scores = lax.dot_general(
            b_t, c_t, (((0,), (0,)), ((), ())), preferred_element_type=jnp.float32
        )
        run = run_ref[j]
        run2 = run * LOG2E
        columns = jnp.transpose(col_ref[j])
        start = local_ref[j] + before * rows_of_heads(jnp.exp(cum_ref[j]), heads)
        carried = jnp.dot(start.astype(jnp.bfloat16), c_t, preferred_element_type=jnp.float32)
        grown = jnp.exp(run)
        squares = jnp.zeros((P_SIZE, CHUNK), jnp.float32)
        for h in range(heads):
            part = slice(h * P_SIZE, (h + 1) * P_SIZE)
            spread = run2[h : h + 1, :] - columns[:, h : h + 1]
            weights = jnp.where(lower, scores * jnp.exp2(spread), 0.0).astype(jnp.bfloat16)
            x_t = xbc_ref[j, part, :]
            own = jnp.dot(x_t, weights, preferred_element_type=jnp.float32)
            y = own + carried[part, :] * grown[h : h + 1, :]
            gate = gate_ref[part, :].astype(jnp.float32)
            opened = gate * (0.5 * jnp.tanh(0.5 * gate) + 0.5)
            u = (y + skip_ref[h] * x_t.astype(jnp.float32)) * opened
            squares = squares + u * u
            u_ref[part, :] = u
        mean = jnp.sum(squares, axis=0, keepdims=True) * (1.0 / width)
        hidden = u_ref[...] * lax.rsqrt(mean + 1e-05) * gain
        hidden_ref[place * CHUNK : (place + 1) * CHUNK, :] = jnp.transpose(
            hidden.astype(jnp.bfloat16)
        )
    w = w_ref[...]
    for at, (tall, out_ref) in enumerate(zip(halves, outs)):
        low = sum(halves[:at])
        out_ref[...] = jnp.dot(
            hidden_ref[low : low + tall, :], w, preferred_element_type=jnp.float32
        ).astype(jnp.bfloat16)


def finish(group, halves, me, skip, arrays, xbc, run, col, cum, local, state, gain, w_out):
    count = len(group)
    width, out_width = w_out.shape
    heads = width // P_SIZE
    operands = [*arrays, xbc, run, col, cum, local, state, gain, w_out]
    results = [jax.ShapeDtypeStruct((tall, out_width), jnp.bfloat16) for tall in halves]
    return pl.pallas_call(
        functools.partial(finish_kernel, heads, group, halves),
        grid=(1,),
        in_specs=[pl.BlockSpec(memory_space=pltpu.SMEM)] * 2 + whole(*operands),
        out_specs=whole(*results),
        out_shape=results,
        scratch_shapes=[
            pltpu.VMEM((count * CHUNK, width), jnp.bfloat16),
            pltpu.VMEM((width, CHUNK), jnp.float32),
        ],
        compiler_params=pltpu.CompilerParams(vmem_limit_bytes=VMEM_LIMIT),
        cost_estimate=pl.CostEstimate(
            flops=2 * count * CHUNK * width * (out_width + 2 * N),
            bytes_accessed=2 * width * out_width + count * 1024 * 1024,
            transcendentals=count * CHUNK * CHUNK * heads,
        ),
        name="finish",
    )(me, skip, *operands)


def add_kernel(*refs):
    total = refs[0][...].astype(jnp.float32)
    for ref in refs[1:-1]:
        total = total + ref[...].astype(jnp.float32)
    refs[-1][...] = total.astype(jnp.bfloat16)


def plus(moving, blocks, at):
    tall, wide = moving[0].shape
    return pl.pallas_call(
        add_kernel,
        grid=(1,),
        in_specs=[pl.BlockSpec((tall, wide), lambda i: (0, 0)) for _ in moving]
        + [pl.BlockSpec((tall, wide), lambda i: (at, 0))],
        out_specs=pl.BlockSpec((tall, wide), lambda i: (0, 0)),
        out_shape=jax.ShapeDtypeStruct((tall, wide), jnp.bfloat16),
        compiler_params=pltpu.CompilerParams(vmem_limit_bytes=VMEM_LIMIT),
        cost_estimate=pl.CostEstimate(
            flops=tall * wide, bytes_accessed=6 * tall * wide, transcendentals=0
        ),
        name="plus",
    )(*moving, blocks)


def per_device(
    tokens, w_in, conv_weight, conv_bias, dt_bias, decay_rate, skip_scale, norm_gain, w_out
):
    me = lax.axis_index("tp")
    n_tp = lax.axis_size("tp")
    width = norm_gain.shape[0]
    heads = decay_rate.shape[0]
    rows = tokens.shape[0] * n_tp
    half = tokens.shape[0] // 2
    w_t = jnp.transpose(w_in.reshape(w_in.shape[0], w_in.shape[2]))
    xbc_width = conv_weight.shape[2]

    def spread_out(taps, bias, per_head):
        return (
            jnp.broadcast_to(
                taps.reshape(taps.shape[0], xbc_width, 1).astype(jnp.float32),
                (taps.shape[0], xbc_width, CHUNK),
            ),
            jnp.broadcast_to(
                bias.reshape(xbc_width, 1).astype(jnp.float32), (xbc_width, CHUNK)
            ),
            jnp.broadcast_to(jnp.stack(per_head)[:, :, None], (2, heads, CHUNK)),
        )

    place = me.astype(jnp.int32).reshape(1)

    right = [tokens[:half], tokens[half:]]
    left = [tokens[:half], tokens[half:]]
    edges = {0: tokens[-8:]}
    arrays = []
    for hop in range(1, 4):
        right = [turned(right[0], "tp", 1), turned(right[1], "tp", 1)]
        left = [turned(left[0], "tp", -1), turned(left[1], "tp", -1)]
        if hop == 1:
            edge, conv_weight, conv_bias, dt_bias, decay_rate, _ = lax.optimization_barrier(
                (edges[0], conv_weight, conv_bias, dt_bias, decay_rate, right[1])
            )
            edges[4] = turned(edge, "tp", -4)
            taps, bias, head_values = spread_out(conv_weight, conv_bias, [dt_bias, decay_rate])
        arrays.append(project(left + right, w_t))
        edges[hop], edges[n_tp - hop] = left[1][-8:], right[1][-8:]
    last = [turned(right[0], "tp", 1), turned(left[1], "tp", -1)]
    arrays.append(project([tokens] + last, w_t))

    edge = edges[0]
    for distance in range(1, n_tp):
        edge = jnp.where((me + distance) % n_tp == n_tp - 1, edges[distance], edge)
    edge = jnp.pad(next_block(edge), ((CHUNK - 8, 0), (0, 0)))
    halo = project([edge], w_t[width : width + xbc_width])

    xbc, run, col, cum, local, payload = chunk_states(
        place, arrays, halo, taps, bias, head_values
    )
    got = lax.all_to_all(payload, "ctx", 0, 0, tiled=True)
    state = lax.all_to_all(prefix(got), "ctx", 0, 0, tiled=True).reshape(width, N)

    shared = (xbc, run, col, cum, local, state, norm_gain.reshape(width // N, N), w_out)
    sent_r0, sent_l1, three, minus_three = finish(
        FIRST_SENT, (half, half, 2 * half, 2 * half), place, skip_scale, arrays, *shared
    )
    (later,) = finish(
        LATER_SENT, (len(LATER_SENT) * 2 * half,), place, skip_scale, arrays, *shared
    )

    def block(distance, part):
        if distance == 3:
            return three, part
        if distance == -3:
            return minus_three, part
        return later, 2 * LATER_SENT.index(distance) + part

    r0, l1 = turned(sent_r0, "tp", 1), turned(sent_l1, "tp", -1)
    r1, l0 = turned(three[half:], "tp", 1), turned(minus_three[:half], "tp", -1)
    for k in (3, 2, 1):
        r0 = turned(plus([r0], *block(k, 0)), "tp", 1)
        l1 = turned(plus([l1], *block(-k, 1)), "tp", -1)
        if k > 1:
            r1 = turned(plus([r1], *block(k - 1, 1)), "tp", 1)
            l0 = turned(plus([l0], *block(1 - k, 0)), "tp", -1)
    top, bottom = plus([r0, l0], *block(0, 0)), plus([r1, l1], *block(0, 1))
    return jnp.concatenate([top, bottom], axis=0)


def solution(mesh):
    placed = (
        P(("ctx", "tp"), None),
        P(None, "tp", None),
        P(None, "tp", None),
        P("tp", None),
        P("tp"),
        P("tp"),
        P("tp"),
        P("tp"),
        P("tp", None),
    )
    return jax.shard_map(
        per_device, mesh=mesh, in_specs=placed, out_specs=P(("ctx", "tp"), None), check_vma=False
    )
```

```python
import functools
import math

import jax
import jax.numpy as jnp
from jax import lax
from jax.experimental import pallas as pl
from jax.experimental.pallas import tpu as pltpu
from jax.sharding import PartitionSpec as P

P_SIZE = 64
N = 128
CHUNK = 128
LOG2E = math.log2(math.e)
VMEM_LIMIT = 36 * 1024 * 1024

PLACE_OF_DISTANCE = ((2, 0), (0, 0), (0, 2), (1, 0), (2, 1), (1, 1), (0, 3), (0, 1))
ARRAYS = 3
GROUPS = ((4, 3, -3), (2, -2), (1, -1, 0))


def turned(value, axis, steps):
    count = lax.axis_size(axis)
    return lax.ppermute(value, axis, [(i, (i + steps) % count) for i in range(count)])


def next_block(value, steps):
    blocks, count = lax.axis_size("ctx"), lax.axis_size("tp")
    return lax.ppermute(
        value,
        ("ctx", "tp"),
        [
            (c * count + t, (c + 1) * count + (t + steps) % count)
            for c in range(blocks - 1)
            for t in range(count)
        ],
    )


def after(value, *earlier):
    return lax.optimization_barrier((value, *earlier))[0]


def rows_of_heads(per_head, heads):
    width = per_head.shape[1]
    return jnp.concatenate(
        [jnp.broadcast_to(per_head[h : h + 1], (P_SIZE, width)) for h in range(heads)], axis=0
    )


def project(pieces, w_t):
    rows = jnp.concatenate(pieces, axis=0) if len(pieces) > 1 else pieces[0]
    return lax.dot_general(
        w_t, rows, (((1,), (1,)), ((), ())), preferred_element_type=jnp.float32
    ).astype(jnp.bfloat16)


def chunk_of(arrays, distance):
    which, side = PLACE_OF_DISTANCE[distance]
    return arrays[which].at[:, side * CHUNK : (side + 1) * CHUNK]


def whole(*shapes):
    def zeros(rank):
        return lambda i: (0,) * rank

    return [pl.BlockSpec(tuple(item.shape), zeros(len(item.shape))) for item in shapes]


def lanes_kernel(taps_ref, bias_ref, head_ref, wide_ref, wide_head_ref):
    count = taps_ref.shape[0]
    for at in range(0, taps_ref.shape[1], N):
        part = slice(at, at + N)
        columns = jnp.transpose(
            jnp.concatenate(
                [
                    taps_ref[:, part].astype(jnp.float32),
                    bias_ref[:, part].astype(jnp.float32),
                    jnp.zeros((7 - count, N), jnp.float32),
                ],
                axis=0,
            )
        )
        for k in range(count + 1):
            wide_ref[k, part, :] = jnp.broadcast_to(columns[:, k : k + 1], (N, CHUNK))
    heads = jnp.transpose(head_ref[...])
    for k in range(head_ref.shape[0]):
        wide_head_ref[k] = jnp.broadcast_to(heads[:, k : k + 1], wide_head_ref.shape[1:])


def along_lanes(taps, bias, head_values):
    results = [
        jax.ShapeDtypeStruct((taps.shape[0] + 1, taps.shape[1], CHUNK), jnp.float32),
        jax.ShapeDtypeStruct((*head_values.shape, CHUNK), jnp.float32),
    ]
    return pl.pallas_call(
        lanes_kernel,
        grid=(1,),
        in_specs=whole(taps, bias, head_values),
        out_specs=whole(*results),
        out_shape=results,
        compiler_params=pltpu.CompilerParams(vmem_limit_bytes=8 * 1024 * 1024),
        name="along_lanes",
    )(taps, bias, head_values)


def convolve(raw, before, taps_ref, at):
    part = pl.ds(at, P_SIZE)
    lanes = lax.broadcasted_iota(jnp.int32, raw.shape, 1)
    acc = taps_ref[4, part, :] + raw * taps_ref[3, part, :]
    for back in (1, 2, 3):
        moved = jnp.where(lanes < back, pltpu.roll(before, back, 1), pltpu.roll(raw, back, 1))
        acc = acc + moved * taps_ref[3 - back, part, :]
    return (acc * (0.5 * jnp.tanh(0.5 * acc) + 0.5)).astype(jnp.bfloat16)


def added_state(xbc, factor, heads):
    width = heads * P_SIZE
    inflow = (xbc[:width].astype(jnp.float32) * rows_of_heads(factor, heads)).astype(jnp.bfloat16)
    return lax.dot_general(
        inflow,
        xbc[width : width + N],
        (((1,), (1,)), ((), ())),
        preferred_element_type=jnp.float32,
    )


def inputs_kernel(heads, chunks, me_ref, *refs):
    arrays = refs[:ARRAYS]
    taps_ref, head_ref = refs[ARRAYS : ARRAYS + 2]
    xbc_ref, run_ref, col_ref, cum_ref, factor_ref, keep_ref = refs[ARRAYS + 2 : ARRAYS + 8]
    raw_ref, dt_ref = refs[ARRAYS + 8 :]
    width = heads * P_SIZE
    xbc_width = xbc_ref.shape[1]
    me = me_ref[0]
    for distance in range(chunks):
        j = lax.rem(me + distance, chunks)
        source = chunk_of(arrays, distance)
        raw_ref[j] = source[width : width + xbc_width, :]
        dt_ref[j] = source[width + xbc_width : width + xbc_width + heads, :].astype(jnp.float32)

    shifted = dt_ref[...] + head_ref[0]
    dt = jnp.maximum(shifted, 0.0) + jnp.log1p(jnp.exp(-jnp.abs(shifted)))
    run = (-head_ref[1] * dt).reshape(chunks * heads, CHUNK)
    lanes = lax.broadcasted_iota(jnp.int32, run.shape, 1)
    reach = 1
    while reach < CHUNK:
        run = run + jnp.where(lanes >= reach, pltpu.roll(run, reach, 1), 0.0)
        reach *= 2
    run = run.reshape(chunks, heads, CHUNK)
    total = jnp.broadcast_to(run[:, :, CHUNK - 1 :], run.shape)
    run_ref[...] = run
    col_ref[...] = run * LOG2E - jnp.log2(dt)
    factor_ref[...] = jnp.exp(total - run) * dt
    keep_ref[...] = jnp.exp(total)
    cum = jnp.zeros((heads, CHUNK), jnp.float32)
    for j in range(chunks):
        cum_ref[j] = cum
        cum = cum + total[j]
    cum_ref[chunks] = cum
    for j in range(1, chunks):
        for at in range(0, xbc_width, P_SIZE):
            part = pl.ds(at, P_SIZE)
            xbc_ref[j - 1, part, :] = convolve(
                raw_ref[j, part, :].astype(jnp.float32),
                raw_ref[j - 1, part, :].astype(jnp.float32),
                taps_ref,
                at,
            )


def chunk_inputs(me, arrays, taps, head_values):
    heads = head_values.shape[1]
    xbc_width = taps.shape[1]
    rows = sum(array.shape[1] for array in arrays)
    chunks = rows // CHUNK
    operands = [*arrays, taps, head_values]
    small = jax.ShapeDtypeStruct((chunks, heads, CHUNK), jnp.float32)
    results = [
        jax.ShapeDtypeStruct((chunks - 1, xbc_width, CHUNK), jnp.bfloat16),
        small,
        small,
        jax.ShapeDtypeStruct((chunks + 1, heads, CHUNK), jnp.float32),
        small,
        small,
    ]
    return pl.pallas_call(
        functools.partial(inputs_kernel, heads, chunks),
        grid=(1,),
        in_specs=[pl.BlockSpec(memory_space=pltpu.SMEM)] + whole(*operands),
        out_specs=whole(*results),
        out_shape=results,
        scratch_shapes=[
            pltpu.VMEM((chunks, xbc_width, CHUNK), jnp.bfloat16),
            pltpu.VMEM((chunks, heads, CHUNK), jnp.float32),
        ],
        compiler_params=pltpu.CompilerParams(vmem_limit_bytes=VMEM_LIMIT),
        cost_estimate=pl.CostEstimate(
            flops=30 * rows * xbc_width,
            bytes_accessed=8 * 1024 * 1024,
            transcendentals=2 * rows * xbc_width,
        ),
        name="chunk_inputs",
    )(me, *operands)


def states_kernel(heads, chunks, me_ref, *refs):
    arrays = refs[:ARRAYS]
    halo_ref, later_ref, taps_ref, cum_ref, factor_ref, keep_ref = refs[ARRAYS : ARRAYS + 6]
    xbc_ref, local_ref, payload_ref, raw_ref = refs[ARRAYS + 6 :]
    width = heads * P_SIZE
    xbc_width = xbc_ref.shape[1]
    for distance in range(chunks):

        @pl.when(lax.rem(me_ref[0] + distance, chunks) == 0)
        def _():
            raw_ref[...] = chunk_of(arrays, distance)[width : width + xbc_width, :]

    for at in range(0, xbc_width, P_SIZE):
        part = pl.ds(at, P_SIZE)
        xbc_ref[0, part, :] = convolve(
            raw_ref[part, :].astype(jnp.float32),
            halo_ref[part, :].astype(jnp.float32),
            taps_ref,
            at,
        )
    state = jnp.zeros((width, N), jnp.float32)
    for j in range(chunks):
        if j:
            xbc_ref[j] = later_ref[j - 1]
        local_ref[j] = state
        added = added_state(later_ref[j - 1] if j else xbc_ref[0], factor_ref[j], heads)
        state = state * rows_of_heads(keep_ref[j], heads) + added if j else added

    row = lax.broadcasted_iota(jnp.int32, (16, N), 0)
    all_keep = jnp.exp(cum_ref[chunks])
    high = all_keep.astype(jnp.bfloat16).astype(jnp.float32)
    mid = (all_keep - high).astype(jnp.bfloat16).astype(jnp.float32)
    low = all_keep - high - mid
    for piece in range(width // 16):
        h = piece * 16 // P_SIZE
        payload_ref[piece, :16, :] = state[piece * 16 : piece * 16 + 16].astype(jnp.bfloat16)
        parts = jnp.where(
            row == 0,
            jnp.broadcast_to(high[h : h + 1], (16, N)),
            jnp.where(
                row == 1,
                jnp.broadcast_to(mid[h : h + 1], (16, N)),
                jnp.broadcast_to(low[h : h + 1], (16, N)),
            ),
        )
        payload_ref[piece, 16:, :] = parts.astype(jnp.bfloat16)


def chunk_states(me, arrays, halo, later, taps, cum, factor, keep):
    heads = factor.shape[1]
    width = heads * P_SIZE
    xbc_width = taps.shape[1]
    chunks = factor.shape[0]
    operands = [*arrays, halo, later, taps, cum, factor, keep]
    results = [
        jax.ShapeDtypeStruct((chunks, xbc_width, CHUNK), jnp.bfloat16),
        jax.ShapeDtypeStruct((chunks, width, N), jnp.float32),
        jax.ShapeDtypeStruct((width // 16, 32, N), jnp.bfloat16),
    ]
    return pl.pallas_call(
        functools.partial(states_kernel, heads, chunks),
        grid=(1,),
        in_specs=[pl.BlockSpec(memory_space=pltpu.SMEM)] + whole(*operands),
        out_specs=whole(*results),
        out_shape=results,
        scratch_shapes=[pltpu.VMEM((xbc_width, CHUNK), jnp.bfloat16)],
        compiler_params=pltpu.CompilerParams(vmem_limit_bytes=VMEM_LIMIT),
        cost_estimate=pl.CostEstimate(
            flops=2 * chunks * CHUNK * width * N,
            bytes_accessed=8 * 1024 * 1024,
            transcendentals=CHUNK * xbc_width,
        ),
        name="chunk_states",
    )(me, *operands)


def prefix_kernel(got_ref, out_ref):
    count = got_ref.shape[0]
    tails = [got_ref[c, 16:, :].astype(jnp.float32) for c in range(count - 1)]
    keeps = [jnp.broadcast_to(tail[0:1] + tail[1:2] + tail[2:3], (16, N)) for tail in tails]
    state = jnp.zeros((16, N), jnp.float32)
    for c in range(count):
        out_ref[c] = state.astype(jnp.bfloat16)
        if c < count - 1:
            state = state * keeps[c] + got_ref[c, :16, :].astype(jnp.float32)


def prefix(got):
    count = got.shape[0]
    return pl.pallas_call(
        prefix_kernel,
        out_shape=jax.ShapeDtypeStruct((count, 16, N), jnp.bfloat16),
        compiler_params=pltpu.CompilerParams(vmem_limit_bytes=4 * 1024 * 1024),
        name="prefix",
    )(got)


def finish_kernel(heads, group, halves, me_ref, skip_ref, *refs):
    arrays = refs[:ARRAYS]
    xbc_ref, run_ref, col_ref, cum_ref, local_ref = refs[ARRAYS : ARRAYS + 5]
    state_ref, gain_ref, w_ref = refs[ARRAYS + 5 : ARRAYS + 8]
    outs = refs[ARRAYS + 8 : -2]
    hidden_ref, u_ref = refs[-2:]
    width = heads * P_SIZE
    count = len(PLACE_OF_DISTANCE)
    sender = lax.broadcasted_iota(jnp.int32, (CHUNK, CHUNK), 0)
    taker = lax.broadcasted_iota(jnp.int32, (CHUNK, CHUNK), 1)
    lower = sender <= taker
    before = state_ref[...].astype(jnp.float32)
    gains = jnp.transpose(gain_ref[...])
    gain = jnp.concatenate(
        [jnp.broadcast_to(gains[:, k : k + 1], (N, CHUNK)) for k in range(width // N)], axis=0
    )
    for place, distance in enumerate(group):
        j = lax.rem(me_ref[0] + distance + count, count)
        gate_ref = chunk_of(arrays, distance % count)
        b_t = xbc_ref[j, width : width + N, :]
        c_t = xbc_ref[j, width + N : width + 2 * N, :]
        scores = lax.dot_general(
            b_t, c_t, (((0,), (0,)), ((), ())), preferred_element_type=jnp.float32
        )
        run = run_ref[j]
        run2 = run * LOG2E
        columns = jnp.transpose(col_ref[j])
        start = local_ref[j] + before * rows_of_heads(jnp.exp(cum_ref[j]), heads)
        carried = jnp.dot(start.astype(jnp.bfloat16), c_t, preferred_element_type=jnp.float32)
        grown = jnp.exp(run)
        squares = jnp.zeros((P_SIZE, CHUNK), jnp.float32)
        for h in range(heads):
            part = slice(h * P_SIZE, (h + 1) * P_SIZE)
            spread = run2[h : h + 1, :] - columns[:, h : h + 1]
            weights = jnp.where(lower, scores * jnp.exp2(spread), 0.0).astype(jnp.bfloat16)
            x_t = xbc_ref[j, part, :]
            own = jnp.dot(x_t, weights, preferred_element_type=jnp.float32)
            y = own + carried[part, :] * grown[h : h + 1, :]
            gate = gate_ref[part, :].astype(jnp.float32)
            opened = gate * (0.5 * jnp.tanh(0.5 * gate) + 0.5)
            u = (y + skip_ref[h] * x_t.astype(jnp.float32)) * opened
            squares = squares + u * u
            u_ref[part, :] = u
        mean = jnp.sum(squares, axis=0, keepdims=True) * (1.0 / width)
        hidden = u_ref[...] * lax.rsqrt(mean + 1e-05) * gain
        hidden_ref[place * CHUNK : (place + 1) * CHUNK, :] = jnp.transpose(
            hidden.astype(jnp.bfloat16)
        )
    w = w_ref[...]
    for at, (tall, out_ref) in enumerate(zip(halves, outs)):
        low = sum(halves[:at])
        out_ref[...] = jnp.dot(
            hidden_ref[low : low + tall, :], w, preferred_element_type=jnp.float32
        ).astype(jnp.bfloat16)


def finish(group, halves, me, skip, arrays, xbc, run, col, cum, local, state, gain, w_out):
    count = len(group)
    width, out_width = w_out.shape
    heads = width // P_SIZE
    operands = [*arrays, xbc, run, col, cum, local, state, gain, w_out]
    results = [jax.ShapeDtypeStruct((tall, out_width), jnp.bfloat16) for tall in halves]
    return pl.pallas_call(
        functools.partial(finish_kernel, heads, group, halves),
        grid=(1,),
        in_specs=[pl.BlockSpec(memory_space=pltpu.SMEM)] * 2 + whole(*operands),
        out_specs=whole(*results),
        out_shape=results,
        scratch_shapes=[
            pltpu.VMEM((count * CHUNK, width), jnp.bfloat16),
            pltpu.VMEM((width, CHUNK), jnp.float32),
        ],
        compiler_params=pltpu.CompilerParams(vmem_limit_bytes=VMEM_LIMIT),
        cost_estimate=pl.CostEstimate(
            flops=2 * count * CHUNK * width * (out_width + 2 * N),
            bytes_accessed=2 * width * out_width + count * 1024 * 1024,
            transcendentals=count * CHUNK * CHUNK * heads,
        ),
        name="finish",
    )(me, skip, *operands)


def add_kernel(*refs):
    total = refs[0][...].astype(jnp.float32)
    for ref in refs[1:-1]:
        total = total + ref[...].astype(jnp.float32)
    refs[-1][...] = total.astype(jnp.bfloat16)


def plus(moving, blocks, at):
    tall, wide = moving[0].shape
    return pl.pallas_call(
        add_kernel,
        grid=(1,),
        in_specs=[pl.BlockSpec((tall, wide), lambda i: (0, 0)) for _ in moving]
        + [pl.BlockSpec((tall, wide), lambda i: (at, 0))],
        out_specs=pl.BlockSpec((tall, wide), lambda i: (0, 0)),
        out_shape=jax.ShapeDtypeStruct((tall, wide), jnp.bfloat16),
        compiler_params=pltpu.CompilerParams(vmem_limit_bytes=8 * 1024 * 1024),
        cost_estimate=pl.CostEstimate(
            flops=tall * wide, bytes_accessed=6 * tall * wide, transcendentals=0
        ),
        name="plus",
    )(*moving, blocks)


def last_kernel(r0_ref, l0_ref, r1_ref, l1_ref, own_ref, out_ref):
    half = r0_ref.shape[0]
    for at, (right, left) in enumerate(((r0_ref, l0_ref), (r1_ref, l1_ref))):
        part = slice(at * half, (at + 1) * half)
        out_ref[part, :] = (
            right[...].astype(jnp.float32)
            + left[...].astype(jnp.float32)
            + own_ref[part, :].astype(jnp.float32)
        ).astype(jnp.bfloat16)


def last_sum(moving, blocks, at):
    tall, wide = moving[0].shape
    return pl.pallas_call(
        last_kernel,
        grid=(1,),
        in_specs=[pl.BlockSpec((tall, wide), lambda i: (0, 0)) for _ in moving]
        + [pl.BlockSpec((2 * tall, wide), lambda i: (at, 0))],
        out_specs=pl.BlockSpec((2 * tall, wide), lambda i: (0, 0)),
        out_shape=jax.ShapeDtypeStruct((2 * tall, wide), jnp.bfloat16),
        compiler_params=pltpu.CompilerParams(vmem_limit_bytes=8 * 1024 * 1024),
        name="last_sum",
    )(*moving, blocks)


def per_device(
    tokens, w_in, conv_weight, conv_bias, dt_bias, decay_rate, skip_scale, norm_gain, w_out
):
    me = lax.axis_index("tp")
    n_tp = lax.axis_size("tp")
    width = norm_gain.shape[0]
    heads = decay_rate.shape[0]
    rows = tokens.shape[0] * n_tp
    half = tokens.shape[0] // 2
    w_t = jnp.transpose(w_in.reshape(w_in.shape[0], w_in.shape[2]))
    xbc_width = conv_weight.shape[2]

    place = me.astype(jnp.int32).reshape(1)

    right = [tokens[:half], tokens[half:]]
    left = [tokens[:half], tokens[half:]]
    edges = {0: tokens[-8:]}
    arrays, pieces = [], []
    for hop in range(1, 4):
        right = [turned(right[0], "tp", 1), turned(right[1], "tp", 1)]
        left = [turned(left[0], "tp", -1), turned(left[1], "tp", -1)]
        edges[hop], edges[n_tp - hop] = left[1][-8:], right[1][-8:]
        pieces += left + right
        if hop == 2:
            arrays.append(project(pieces, w_t))
            pieces = []
            conv_weight, conv_bias, dt_bias, decay_rate, arrays[0] = lax.optimization_barrier(
                (conv_weight, conv_bias, dt_bias, decay_rate, arrays[0])
            )
            taps, head_values = along_lanes(
                conv_weight.reshape(conv_weight.shape[0], xbc_width),
                conv_bias,
                jnp.stack([dt_bias, decay_rate]),
            )
    last = [turned(right[0], "tp", 1), turned(left[1], "tp", -1)]
    arrays.append(project(pieces, w_t))

    edges[4] = last[1][-8:]
    edge = edges[0]
    for distance in range(1, n_tp):
        edge = jnp.where((me + distance) % n_tp == n_tp - 1, edges[distance], edge)
    edge = next_block(edge, 0)
    arrays.append(project([tokens] + last, w_t))
    padding = jnp.zeros((CHUNK - edge.shape[0], edge.shape[1]), edge.dtype)
    halo = project([padding, edge], w_t[width : width + xbc_width])

    later, run, col, cum, factor, keep = chunk_inputs(place, arrays, taps, head_values)
    xbc, local, payload = chunk_states(place, arrays, halo, later, taps, cum, factor, keep)
    got = lax.all_to_all(payload, "ctx", 0, 0, tiled=True)
    state = lax.all_to_all(prefix(got), "ctx", 0, 0, tiled=True).reshape(width, N)

    shared = (xbc, run, col, cum, local, state, norm_gain.reshape(width // N, N), w_out)
    blocks = {}
    for group in GROUPS:
        tall = (half, half) if group[0] == 4 else ()
        tall += (2 * half * (len(group) - len(tall) // 2),)
        made = finish(group, tall, place, skip_scale, arrays, *shared)
        for at, distance in enumerate(group):
            blocks[distance] = (made, at)

    def block(distance, part):
        made, at = blocks[distance]
        return made[-1], 2 * (at - len(made) // 2) + part

    r0, l1 = turned(blocks[4][0][0], "tp", 1), turned(blocks[4][0][1], "tp", -1)
    threes = blocks[3][0][-1]
    r1 = turned(threes[half : 2 * half], "tp", 1)
    l0 = turned(threes[2 * half : 3 * half], "tp", -1)
    for k in (3, 2, 1):
        r0 = turned(plus([r0], *block(k, 0)), "tp", 1)
        l1 = turned(plus([l1], *block(-k, 1)), "tp", -1)
        if k > 1:
            r1 = turned(plus([r1], *block(k - 1, 1)), "tp", 1)
            l0 = turned(plus([l0], *block(1 - k, 0)), "tp", -1)
    return last_sum([r0, l0, r1, l1], blocks[0][0][-1], blocks[0][1])


def solution(mesh):
    placed = (
        P(("ctx", "tp"), None),
        P(None, "tp", None),
        P(None, "tp", None),
        P("tp", None),
        P("tp"),
        P("tp"),
        P("tp"),
        P("tp"),
        P("tp", None),
    )
    return jax.shard_map(
        per_device, mesh=mesh, in_specs=placed, out_specs=P(("ctx", "tp"), None), check_vma=False
    )
```

```python
import functools
import math

import jax
import jax.numpy as jnp
from jax import lax
from jax.experimental import pallas as pl
from jax.experimental.pallas import tpu as pltpu
from jax.sharding import PartitionSpec as P

P_SIZE = 64
N = 128
CHUNK = 128
LOG2E = math.log2(math.e)
VMEM_LIMIT = 36 * 1024 * 1024

PLACE_OF_DISTANCE = ((2, 0), (0, 0), (0, 2), (1, 0), (2, 1), (1, 1), (0, 3), (0, 1))
ARRAYS = 3
GROUPS = ((4, 3, -3), (2, -2), (1, -1, 0))


def turned(value, axis, steps):
    count = lax.axis_size(axis)
    return lax.ppermute(value, axis, [(i, (i + steps) % count) for i in range(count)])


def next_block(value, steps):
    blocks, count = lax.axis_size("ctx"), lax.axis_size("tp")
    return lax.ppermute(
        value,
        ("ctx", "tp"),
        [
            (c * count + t, (c + 1) * count + (t + steps) % count)
            for c in range(blocks - 1)
            for t in range(count)
        ],
    )


def after(value, *earlier):
    return lax.optimization_barrier((value, *earlier))[0]


def rows_of_heads(per_head, heads):
    width = per_head.shape[1]
    return jnp.concatenate(
        [jnp.broadcast_to(per_head[h : h + 1], (P_SIZE, width)) for h in range(heads)], axis=0
    )


def project(pieces, w_t):
    rows = jnp.concatenate(pieces, axis=0) if len(pieces) > 1 else pieces[0]
    return lax.dot_general(
        w_t, rows, (((1,), (1,)), ((), ())), preferred_element_type=jnp.float32
    ).astype(jnp.bfloat16)


def resident_kernel(from_ref, to_ref):
    to_ref[...] = from_ref[...]


def resident(array):
    rows, columns = array.shape
    tile = 256
    return pl.pallas_call(
        resident_kernel,
        grid=(pl.cdiv(rows, tile),),
        in_specs=[pl.BlockSpec((tile, columns), lambda i: (i, 0))],
        out_specs=pl.BlockSpec((tile, columns), lambda i: (i, 0)),
        out_shape=jax.ShapeDtypeStruct(array.shape, array.dtype),
        compiler_params=pltpu.CompilerParams(vmem_limit_bytes=8 * 1024 * 1024),
        name="resident",
    )(array)


def chunk_of(arrays, distance):
    which, side = PLACE_OF_DISTANCE[distance]
    return arrays[which].at[:, side * CHUNK : (side + 1) * CHUNK]


def whole(*shapes):
    def zeros(rank):
        return lambda i: (0,) * rank

    return [pl.BlockSpec(tuple(item.shape), zeros(len(item.shape))) for item in shapes]


def lanes_kernel(taps_ref, bias_ref, head_ref, wide_ref, wide_head_ref):
    count = taps_ref.shape[0]
    for at in range(0, taps_ref.shape[1], N):
        part = slice(at, at + N)
        columns = jnp.transpose(
            jnp.concatenate(
                [
                    taps_ref[:, part].astype(jnp.float32),
                    bias_ref[:, part].astype(jnp.float32),
                    jnp.zeros((7 - count, N), jnp.float32),
                ],
                axis=0,
            )
        )
        for k in range(count + 1):
            wide_ref[k, part, :] = jnp.broadcast_to(columns[:, k : k + 1], (N, CHUNK))
    heads = jnp.transpose(head_ref[...])
    for k in range(head_ref.shape[0]):
        wide_head_ref[k] = jnp.broadcast_to(heads[:, k : k + 1], wide_head_ref.shape[1:])


def along_lanes(taps, bias, head_values):
    results = [
        jax.ShapeDtypeStruct((taps.shape[0] + 1, taps.shape[1], CHUNK), jnp.float32),
        jax.ShapeDtypeStruct((*head_values.shape, CHUNK), jnp.float32),
    ]
    return pl.pallas_call(
        lanes_kernel,
        grid=(1,),
        in_specs=whole(taps, bias, head_values),
        out_specs=whole(*results),
        out_shape=results,
        compiler_params=pltpu.CompilerParams(vmem_limit_bytes=8 * 1024 * 1024),
        name="along_lanes",
    )(taps, bias, head_values)


def convolve(raw, before, taps_ref, at):
    part = pl.ds(at, P_SIZE)
    lanes = lax.broadcasted_iota(jnp.int32, raw.shape, 1)
    acc = taps_ref[4, part, :] + raw * taps_ref[3, part, :]
    for back in (1, 2, 3):
        moved = jnp.where(lanes < back, pltpu.roll(before, back, 1), pltpu.roll(raw, back, 1))
        acc = acc + moved * taps_ref[3 - back, part, :]
    return (acc * (0.5 * jnp.tanh(0.5 * acc) + 0.5)).astype(jnp.bfloat16)


def added_state(xbc, factor, heads):
    width = heads * P_SIZE
    inflow = (xbc[:width].astype(jnp.float32) * rows_of_heads(factor, heads)).astype(jnp.bfloat16)
    return lax.dot_general(
        inflow,
        xbc[width : width + N],
        (((1,), (1,)), ((), ())),
        preferred_element_type=jnp.float32,
    )


def inputs_kernel(heads, chunks, me_ref, *refs):
    arrays = refs[:ARRAYS]
    taps_ref, head_ref = refs[ARRAYS : ARRAYS + 2]
    xbc_ref, run_ref, col_ref, cum_ref, factor_ref, keep_ref = refs[ARRAYS + 2 : ARRAYS + 8]
    raw_ref, dt_ref = refs[ARRAYS + 8 :]
    width = heads * P_SIZE
    xbc_width = xbc_ref.shape[1]
    me = me_ref[0]
    for distance in range(chunks):
        j = lax.rem(me + distance, chunks)
        source = chunk_of(arrays, distance)
        raw_ref[j] = source[width : width + xbc_width, :]
        dt_ref[j] = source[width + xbc_width : width + xbc_width + heads, :].astype(jnp.float32)

    shifted = dt_ref[...] + head_ref[0]
    dt = jnp.maximum(shifted, 0.0) + jnp.log1p(jnp.exp(-jnp.abs(shifted)))
    run = (-head_ref[1] * dt).reshape(chunks * heads, CHUNK)
    lanes = lax.broadcasted_iota(jnp.int32, run.shape, 1)
    reach = 1
    while reach < CHUNK:
        run = run + jnp.where(lanes >= reach, pltpu.roll(run, reach, 1), 0.0)
        reach *= 2
    run = run.reshape(chunks, heads, CHUNK)
    total = jnp.broadcast_to(run[:, :, CHUNK - 1 :], run.shape)
    run_ref[...] = run
    col_ref[...] = run * LOG2E - jnp.log2(dt)
    factor_ref[...] = jnp.exp(total - run) * dt
    keep_ref[...] = jnp.exp(total)
    cum = jnp.zeros((heads, CHUNK), jnp.float32)
    for j in range(chunks):
        cum_ref[j] = cum
        cum = cum + total[j]
    cum_ref[chunks] = cum
    for j in range(1, chunks):
        for at in range(0, xbc_width, P_SIZE):
            part = pl.ds(at, P_SIZE)
            xbc_ref[j - 1, part, :] = convolve(
                raw_ref[j, part, :].astype(jnp.float32),
                raw_ref[j - 1, part, :].astype(jnp.float32),
                taps_ref,
                at,
            )


def chunk_inputs(me, arrays, taps, head_values):
    heads = head_values.shape[1]
    xbc_width = taps.shape[1]
    rows = sum(array.shape[1] for array in arrays)
    chunks = rows // CHUNK
    operands = [*arrays, taps, head_values]
    small = jax.ShapeDtypeStruct((chunks, heads, CHUNK), jnp.float32)
    results = [
        jax.ShapeDtypeStruct((chunks - 1, xbc_width, CHUNK), jnp.bfloat16),
        small,
        small,
        jax.ShapeDtypeStruct((chunks + 1, heads, CHUNK), jnp.float32),
        small,
        small,
    ]
    return pl.pallas_call(
        functools.partial(inputs_kernel, heads, chunks),
        grid=(1,),
        in_specs=[pl.BlockSpec(memory_space=pltpu.SMEM)] + whole(*operands),
        out_specs=whole(*results),
        out_shape=results,
        scratch_shapes=[
            pltpu.VMEM((chunks, xbc_width, CHUNK), jnp.bfloat16),
            pltpu.VMEM((chunks, heads, CHUNK), jnp.float32),
        ],
        compiler_params=pltpu.CompilerParams(vmem_limit_bytes=VMEM_LIMIT),
        cost_estimate=pl.CostEstimate(
            flops=30 * rows * xbc_width,
            bytes_accessed=8 * 1024 * 1024,
            transcendentals=2 * rows * xbc_width,
        ),
        name="chunk_inputs",
    )(me, *operands)


def states_kernel(heads, chunks, me_ref, *refs):
    arrays = refs[:ARRAYS]
    halo_ref, later_ref, taps_ref, cum_ref, factor_ref, keep_ref = refs[ARRAYS : ARRAYS + 6]
    xbc_ref, local_ref, payload_ref, raw_ref = refs[ARRAYS + 6 :]
    width = heads * P_SIZE
    xbc_width = xbc_ref.shape[1]
    for distance in range(chunks):

        @pl.when(lax.rem(me_ref[0] + distance, chunks) == 0)
        def _():
            raw_ref[...] = chunk_of(arrays, distance)[width : width + xbc_width, :]

    for at in range(0, xbc_width, P_SIZE):
        part = pl.ds(at, P_SIZE)
        xbc_ref[0, part, :] = convolve(
            raw_ref[part, :].astype(jnp.float32),
            halo_ref[part, :].astype(jnp.float32),
            taps_ref,
            at,
        )
    state = jnp.zeros((width, N), jnp.float32)
    for j in range(chunks):
        if j:
            xbc_ref[j] = later_ref[j - 1]
        local_ref[j] = state
        added = added_state(later_ref[j - 1] if j else xbc_ref[0], factor_ref[j], heads)
        state = state * rows_of_heads(keep_ref[j], heads) + added if j else added

    row = lax.broadcasted_iota(jnp.int32, (16, N), 0)
    all_keep = jnp.exp(cum_ref[chunks])
    high = all_keep.astype(jnp.bfloat16).astype(jnp.float32)
    mid = (all_keep - high).astype(jnp.bfloat16).astype(jnp.float32)
    low = all_keep - high - mid
    for piece in range(width // 16):
        h = piece * 16 // P_SIZE
        payload_ref[piece, :16, :] = state[piece * 16 : piece * 16 + 16].astype(jnp.bfloat16)
        parts = jnp.where(
            row == 0,
            jnp.broadcast_to(high[h : h + 1], (16, N)),
            jnp.where(
                row == 1,
                jnp.broadcast_to(mid[h : h + 1], (16, N)),
                jnp.broadcast_to(low[h : h + 1], (16, N)),
            ),
        )
        payload_ref[piece, 16:, :] = parts.astype(jnp.bfloat16)


def chunk_states(me, arrays, halo, later, taps, cum, factor, keep):
    heads = factor.shape[1]
    width = heads * P_SIZE
    xbc_width = taps.shape[1]
    chunks = factor.shape[0]
    operands = [*arrays, halo, later, taps, cum, factor, keep]
    results = [
        jax.ShapeDtypeStruct((chunks, xbc_width, CHUNK), jnp.bfloat16),
        jax.ShapeDtypeStruct((chunks, width, N), jnp.float32),
        jax.ShapeDtypeStruct((width // 16, 32, N), jnp.bfloat16),
    ]
    return pl.pallas_call(
        functools.partial(states_kernel, heads, chunks),
        grid=(1,),
        in_specs=[pl.BlockSpec(memory_space=pltpu.SMEM)] + whole(*operands),
        out_specs=whole(*results),
        out_shape=results,
        scratch_shapes=[pltpu.VMEM((xbc_width, CHUNK), jnp.bfloat16)],
        compiler_params=pltpu.CompilerParams(vmem_limit_bytes=VMEM_LIMIT),
        cost_estimate=pl.CostEstimate(
            flops=2 * chunks * CHUNK * width * N,
            bytes_accessed=8 * 1024 * 1024,
            transcendentals=CHUNK * xbc_width,
        ),
        name="chunk_states",
    )(me, *operands)


def prefix_kernel(got_ref, out_ref):
    count = got_ref.shape[0]
    tails = [got_ref[c, 16:, :].astype(jnp.float32) for c in range(count - 1)]
    keeps = [jnp.broadcast_to(tail[0:1] + tail[1:2] + tail[2:3], (16, N)) for tail in tails]
    state = jnp.zeros((16, N), jnp.float32)
    for c in range(count):
        out_ref[c] = state.astype(jnp.bfloat16)
        if c < count - 1:
            state = state * keeps[c] + got_ref[c, :16, :].astype(jnp.float32)


def prefix(got):
    count = got.shape[0]
    return pl.pallas_call(
        prefix_kernel,
        out_shape=jax.ShapeDtypeStruct((count, 16, N), jnp.bfloat16),
        compiler_params=pltpu.CompilerParams(vmem_limit_bytes=4 * 1024 * 1024),
        name="prefix",
    )(got)


def finish_kernel(heads, group, halves, me_ref, skip_ref, *refs):
    arrays = refs[:ARRAYS]
    xbc_ref, run_ref, col_ref, cum_ref, local_ref = refs[ARRAYS : ARRAYS + 5]
    state_ref, gain_ref, w_ref = refs[ARRAYS + 5 : ARRAYS + 8]
    outs = refs[ARRAYS + 8 : -2]
    hidden_ref, u_ref = refs[-2:]
    width = heads * P_SIZE
    count = len(PLACE_OF_DISTANCE)
    sender = lax.broadcasted_iota(jnp.int32, (CHUNK, CHUNK), 0)
    taker = lax.broadcasted_iota(jnp.int32, (CHUNK, CHUNK), 1)
    lower = sender <= taker
    before = state_ref[...].astype(jnp.float32)
    gains = jnp.transpose(gain_ref[...])
    gain = jnp.concatenate(
        [jnp.broadcast_to(gains[:, k : k + 1], (N, CHUNK)) for k in range(width // N)], axis=0
    )
    for place, distance in enumerate(group):
        j = lax.rem(me_ref[0] + distance + count, count)
        gate_ref = chunk_of(arrays, distance % count)
        b_t = xbc_ref[j, width : width + N, :]
        c_t = xbc_ref[j, width + N : width + 2 * N, :]
        scores = lax.dot_general(
            b_t, c_t, (((0,), (0,)), ((), ())), preferred_element_type=jnp.float32
        )
        run = run_ref[j]
        run2 = run * LOG2E
        columns = jnp.transpose(col_ref[j])
        start = local_ref[j] + before * rows_of_heads(jnp.exp(cum_ref[j]), heads)
        carried = jnp.dot(start.astype(jnp.bfloat16), c_t, preferred_element_type=jnp.float32)
        grown = jnp.exp(run)
        squares = jnp.zeros((P_SIZE, CHUNK), jnp.float32)
        for h in range(heads):
            part = slice(h * P_SIZE, (h + 1) * P_SIZE)
            spread = run2[h : h + 1, :] - columns[:, h : h + 1]
            weights = jnp.where(lower, scores * jnp.exp2(spread), 0.0).astype(jnp.bfloat16)
            x_t = xbc_ref[j, part, :]
            own = jnp.dot(x_t, weights, preferred_element_type=jnp.float32)
            y = own + carried[part, :] * grown[h : h + 1, :]
            gate = gate_ref[part, :].astype(jnp.float32)
            opened = gate * (0.5 * jnp.tanh(0.5 * gate) + 0.5)
            u = (y + skip_ref[h] * x_t.astype(jnp.float32)) * opened
            squares = squares + u * u
            u_ref[part, :] = u
        mean = jnp.sum(squares, axis=0, keepdims=True) * (1.0 / width)
        hidden = u_ref[...] * lax.rsqrt(mean + 1e-05) * gain
        hidden_ref[place * CHUNK : (place + 1) * CHUNK, :] = jnp.transpose(
            hidden.astype(jnp.bfloat16)
        )
    w = w_ref[...]
    for at, (tall, out_ref) in enumerate(zip(halves, outs)):
        low = sum(halves[:at])
        out_ref[...] = jnp.dot(
            hidden_ref[low : low + tall, :], w, preferred_element_type=jnp.float32
        ).astype(jnp.bfloat16)


def finish(group, halves, me, skip, arrays, xbc, run, col, cum, local, state, gain, w_out):
    count = len(group)
    width, out_width = w_out.shape
    heads = width // P_SIZE
    operands = [*arrays, xbc, run, col, cum, local, state, gain, w_out]
    results = [jax.ShapeDtypeStruct((tall, out_width), jnp.bfloat16) for tall in halves]
    return pl.pallas_call(
        functools.partial(finish_kernel, heads, group, halves),
        grid=(1,),
        in_specs=[pl.BlockSpec(memory_space=pltpu.SMEM)] * 2 + whole(*operands),
        out_specs=whole(*results),
        out_shape=results,
        scratch_shapes=[
            pltpu.VMEM((count * CHUNK, width), jnp.bfloat16),
            pltpu.VMEM((width, CHUNK), jnp.float32),
        ],
        compiler_params=pltpu.CompilerParams(vmem_limit_bytes=VMEM_LIMIT),
        cost_estimate=pl.CostEstimate(
            flops=2 * count * CHUNK * width * (out_width + 2 * N),
            bytes_accessed=2 * width * out_width + count * 1024 * 1024,
            transcendentals=count * CHUNK * CHUNK * heads,
        ),
        name="finish",
    )(me, skip, *operands)


def add_kernel(*refs):
    total = refs[0][...].astype(jnp.float32)
    for ref in refs[1:-1]:
        total = total + ref[...].astype(jnp.float32)
    refs[-1][...] = total.astype(jnp.bfloat16)


def plus(moving, blocks, at):
    tall, wide = moving[0].shape
    return pl.pallas_call(
        add_kernel,
        grid=(1,),
        in_specs=[pl.BlockSpec((tall, wide), lambda i: (0, 0)) for _ in moving]
        + [pl.BlockSpec((tall, wide), lambda i: (at, 0))],
        out_specs=pl.BlockSpec((tall, wide), lambda i: (0, 0)),
        out_shape=jax.ShapeDtypeStruct((tall, wide), jnp.bfloat16),
        compiler_params=pltpu.CompilerParams(vmem_limit_bytes=8 * 1024 * 1024),
        cost_estimate=pl.CostEstimate(
            flops=tall * wide, bytes_accessed=6 * tall * wide, transcendentals=0
        ),
        name="plus",
    )(*moving, blocks)


def last_kernel(r0_ref, l0_ref, r1_ref, l1_ref, own_ref, out_ref):
    half = r0_ref.shape[0]
    for at, (right, left) in enumerate(((r0_ref, l0_ref), (r1_ref, l1_ref))):
        part = slice(at * half, (at + 1) * half)
        out_ref[part, :] = (
            right[...].astype(jnp.float32)
            + left[...].astype(jnp.float32)
            + own_ref[part, :].astype(jnp.float32)
        ).astype(jnp.bfloat16)


def last_sum(moving, blocks, at):
    tall, wide = moving[0].shape
    return pl.pallas_call(
        last_kernel,
        grid=(1,),
        in_specs=[pl.BlockSpec((tall, wide), lambda i: (0, 0)) for _ in moving]
        + [pl.BlockSpec((2 * tall, wide), lambda i: (at, 0))],
        out_specs=pl.BlockSpec((2 * tall, wide), lambda i: (0, 0)),
        out_shape=jax.ShapeDtypeStruct((2 * tall, wide), jnp.bfloat16),
        compiler_params=pltpu.CompilerParams(vmem_limit_bytes=8 * 1024 * 1024),
        name="last_sum",
    )(*moving, blocks)


def per_device(
    tokens, w_in, conv_weight, conv_bias, dt_bias, decay_rate, skip_scale, norm_gain, w_out
):
    me = lax.axis_index("tp")
    n_tp = lax.axis_size("tp")
    width = norm_gain.shape[0]
    heads = decay_rate.shape[0]
    rows = tokens.shape[0] * n_tp
    half = tokens.shape[0] // 2
    w_t = jnp.transpose(w_in.reshape(w_in.shape[0], w_in.shape[2]))
    xbc_width = conv_weight.shape[2]

    place = me.astype(jnp.int32).reshape(1)

    right = [tokens[:half], tokens[half:]]
    left = [tokens[:half], tokens[half:]]
    edges = {0: tokens[-8:]}
    arrays, pieces = [], []
    w_t = resident(w_t)
    for hop in range(1, 4):
        right = [turned(right[0], "tp", 1), turned(right[1], "tp", 1)]
        left = [turned(left[0], "tp", -1), turned(left[1], "tp", -1)]
        edges[hop], edges[n_tp - hop] = left[1][-8:], right[1][-8:]
        pieces += left + right
        if hop == 2:
            arrays.append(project(pieces, w_t))
            pieces = []
            conv_weight, conv_bias, dt_bias, decay_rate, arrays[0] = lax.optimization_barrier(
                (conv_weight, conv_bias, dt_bias, decay_rate, arrays[0])
            )
            taps, head_values = along_lanes(
                conv_weight.reshape(conv_weight.shape[0], xbc_width),
                conv_bias,
                jnp.stack([dt_bias, decay_rate]),
            )
    last = [turned(right[0], "tp", 1), turned(left[1], "tp", -1)]
    arrays.append(project(pieces, w_t))

    edges[4] = last[1][-8:]
    edge = edges[0]
    for distance in range(1, n_tp):
        edge = jnp.where((me + distance) % n_tp == n_tp - 1, edges[distance], edge)
    edge = next_block(edge, 0)
    arrays.append(project([tokens] + last, w_t))
    padding = jnp.zeros((CHUNK - edge.shape[0], edge.shape[1]), edge.dtype)
    halo = project([padding, edge], w_t[width : width + xbc_width])

    later, run, col, cum, factor, keep = chunk_inputs(place, arrays, taps, head_values)
    xbc, local, payload = chunk_states(place, arrays, halo, later, taps, cum, factor, keep)
    got = lax.all_to_all(payload, "ctx", 0, 0, tiled=True)
    state = lax.all_to_all(prefix(got), "ctx", 0, 0, tiled=True).reshape(width, N)

    shared = (xbc, run, col, cum, local, state, norm_gain.reshape(width // N, N), w_out)
    blocks = {}
    for group in GROUPS:
        tall = (half, half) if group[0] == 4 else ()
        tall += (2 * half * (len(group) - len(tall) // 2),)
        made = finish(group, tall, place, skip_scale, arrays, *shared)
        for at, distance in enumerate(group):
            blocks[distance] = (made, at)

    def block(distance, part):
        made, at = blocks[distance]
        return made[-1], 2 * (at - len(made) // 2) + part

    r0, l1 = turned(blocks[4][0][0], "tp", 1), turned(blocks[4][0][1], "tp", -1)
    threes = blocks[3][0][-1]
    r1 = turned(threes[half : 2 * half], "tp", 1)
    l0 = turned(threes[2 * half : 3 * half], "tp", -1)
    for k in (3, 2, 1):
        r0 = turned(plus([r0], *block(k, 0)), "tp", 1)
        l1 = turned(plus([l1], *block(-k, 1)), "tp", -1)
        if k > 1:
            r1 = turned(plus([r1], *block(k - 1, 1)), "tp", 1)
            l0 = turned(plus([l0], *block(1 - k, 0)), "tp", -1)
    return last_sum([r0, l0, r1, l1], blocks[0][0][-1], blocks[0][1])


def solution(mesh):
    placed = (
        P(("ctx", "tp"), None),
        P(None, "tp", None),
        P(None, "tp", None),
        P("tp", None),
        P("tp"),
        P("tp"),
        P("tp"),
        P("tp"),
        P("tp", None),
    )
    return jax.shard_map(
        per_device, mesh=mesh, in_specs=placed, out_specs=P(("ctx", "tp"), None), check_vma=False
    )
```

```python
import functools
import math

import jax
import jax.numpy as jnp
from jax import lax
from jax.experimental import pallas as pl
from jax.experimental.pallas import tpu as pltpu
from jax.sharding import PartitionSpec as P

P_SIZE = 64
N = 128
CHUNK = 128
LOG2E = math.log2(math.e)
VMEM_LIMIT = 36 * 1024 * 1024

PLACE_OF_DISTANCE = ((3, 0), (0, 0), (1, 0), (2, 0), (4, 0), (2, 1), (1, 1), (0, 1))
ARRAYS = 5
HALVES = (0, 1, 1, 0)
EARLY = (-2, -1, 0, 1, 2, 3)
LATE = (4, 5)
GROUPS = ((4, 3, -3), (2, -2), (1, -1, 0))


def turned(value, axis, steps):
    count = lax.axis_size(axis)
    return lax.ppermute(value, axis, [(i, (i + steps) % count) for i in range(count)])


def next_block(value, steps):
    blocks, count = lax.axis_size("ctx"), lax.axis_size("tp")
    return lax.ppermute(
        value,
        ("ctx", "tp"),
        [
            (c * count + t, (c + 1) * count + (t + steps) % count)
            for c in range(blocks - 1)
            for t in range(count)
        ],
    )


def after(value, *earlier):
    return lax.optimization_barrier((value, *earlier))[0]


def rows_of_heads(per_head, heads):
    width = per_head.shape[1]
    return jnp.concatenate(
        [jnp.broadcast_to(per_head[h : h + 1], (P_SIZE, width)) for h in range(heads)], axis=0
    )


def project(pieces, w_t):
    rows = jnp.concatenate(pieces, axis=0) if len(pieces) > 1 else pieces[0]
    return lax.dot_general(
        w_t, rows, (((1,), (1,)), ((), ())), preferred_element_type=jnp.float32
    ).astype(jnp.bfloat16)


def resident_kernel(from_ref, to_ref):
    to_ref[...] = from_ref[...]


def resident(array):
    rows, columns = array.shape
    tile = 256
    return pl.pallas_call(
        resident_kernel,
        grid=(pl.cdiv(rows, tile),),
        in_specs=[pl.BlockSpec((tile, columns), lambda i: (i, 0))],
        out_specs=pl.BlockSpec((tile, columns), lambda i: (i, 0)),
        out_shape=jax.ShapeDtypeStruct(array.shape, array.dtype),
        compiler_params=pltpu.CompilerParams(vmem_limit_bytes=8 * 1024 * 1024),
        name="resident",
    )(array)


def halves_kernel(rows_ref, *out_refs):
    half = rows_ref.shape[0] // 2
    for out_ref, low in zip(out_refs, HALVES):
        out_ref[...] = rows_ref[low * half : (low + 1) * half, :]


def halves(rows):
    tall, wide = rows.shape
    result = jax.ShapeDtypeStruct((tall // 2, wide), rows.dtype)
    return pl.pallas_call(
        halves_kernel,
        grid=(1,),
        in_specs=whole(rows),
        out_specs=whole(*[result] * 4),
        out_shape=[result] * 4,
        compiler_params=pltpu.CompilerParams(vmem_limit_bytes=8 * 1024 * 1024),
        name="halves",
    )(rows)


def chunk_of(arrays, distance, low, high):
    which, side = PLACE_OF_DISTANCE[distance]
    rows = slice(low, high)
    if distance in (0, 4):
        return arrays[which][rows, side * CHUNK : (side + 1) * CHUNK]
    first = arrays[which][rows, :CHUNK].astype(jnp.float32)
    second = arrays[which][rows, CHUNK : 2 * CHUNK].astype(jnp.float32)
    second = pltpu.roll(second, CHUNK // 2, 1)
    upper = lax.broadcasted_iota(jnp.int32, first.shape, 1) < CHUNK // 2
    parts = (second, first) if side == 0 else (first, second)
    return jnp.where(upper, *parts).astype(jnp.bfloat16)


def whole(*shapes):
    def zeros(rank):
        return lambda i: (0,) * rank

    return [pl.BlockSpec(tuple(item.shape), zeros(len(item.shape))) for item in shapes]


def lanes_kernel(taps_ref, bias_ref, head_ref, wide_ref, wide_head_ref):
    count = taps_ref.shape[0]
    for at in range(0, taps_ref.shape[1], N):
        part = slice(at, at + N)
        columns = jnp.transpose(
            jnp.concatenate(
                [
                    taps_ref[:, part].astype(jnp.float32),
                    bias_ref[:, part].astype(jnp.float32),
                    jnp.zeros((7 - count, N), jnp.float32),
                ],
                axis=0,
            )
        )
        for k in range(count + 1):
            wide_ref[k, part, :] = jnp.broadcast_to(columns[:, k : k + 1], (N, CHUNK))
    heads = jnp.transpose(head_ref[...])
    for k in range(head_ref.shape[0]):
        wide_head_ref[k] = jnp.broadcast_to(heads[:, k : k + 1], wide_head_ref.shape[1:])


def along_lanes(taps, bias, head_values):
    results = [
        jax.ShapeDtypeStruct((taps.shape[0] + 1, taps.shape[1], CHUNK), jnp.float32),
        jax.ShapeDtypeStruct((*head_values.shape, CHUNK), jnp.float32),
    ]
    return pl.pallas_call(
        lanes_kernel,
        grid=(1,),
        in_specs=whole(taps, bias, head_values),
        out_specs=whole(*results),
        out_shape=results,
        compiler_params=pltpu.CompilerParams(vmem_limit_bytes=8 * 1024 * 1024),
        name="along_lanes",
    )(taps, bias, head_values)


def convolve(raw, before, taps_ref, at):
    part = pl.ds(at, P_SIZE)
    lanes = lax.broadcasted_iota(jnp.int32, raw.shape, 1)
    acc = taps_ref[4, part, :] + raw * taps_ref[3, part, :]
    for back in (1, 2, 3):
        moved = jnp.where(lanes < back, pltpu.roll(before, back, 1), pltpu.roll(raw, back, 1))
        acc = acc + moved * taps_ref[3 - back, part, :]
    return (acc * (0.5 * jnp.tanh(0.5 * acc) + 0.5)).astype(jnp.bfloat16)


def added_state(xbc, factor, heads):
    width = heads * P_SIZE
    inflow = (xbc[:width].astype(jnp.float32) * rows_of_heads(factor, heads)).astype(jnp.bfloat16)
    return lax.dot_general(
        inflow,
        xbc[width : width + N],
        (((1,), (1,)), ((), ())),
        preferred_element_type=jnp.float32,
    )


def convolve_chunks(raws, distances, taps_ref, xbc_ref):
    for place, distance in enumerate(distances):
        for at in range(0, xbc_ref.shape[1], P_SIZE):
            part = slice(at, at + P_SIZE)
            xbc_ref[place, part, :] = convolve(
                raws[distance][part].astype(jnp.float32),
                raws[distance - 1][part].astype(jnp.float32),
                taps_ref,
                at,
            )


def early_kernel(width, *refs):
    arrays, taps_ref, xbc_ref = refs[: ARRAYS - 1], refs[ARRAYS - 1], refs[ARRAYS]
    xbc_width = xbc_ref.shape[1]
    raws = {
        distance: chunk_of(arrays, distance % 8, width, width + xbc_width)
        for distance in (EARLY[0] - 1, *EARLY)
    }
    convolve_chunks(raws, EARLY, taps_ref, xbc_ref)


def early_chunks(arrays, taps, width):
    xbc_width = taps.shape[1]
    operands = [*arrays, taps]
    result = jax.ShapeDtypeStruct((len(EARLY), xbc_width, CHUNK), jnp.bfloat16)
    return pl.pallas_call(
        functools.partial(early_kernel, width),
        grid=(1,),
        in_specs=whole(*operands),
        out_specs=whole(result)[0],
        out_shape=result,
        compiler_params=pltpu.CompilerParams(vmem_limit_bytes=VMEM_LIMIT),
        cost_estimate=pl.CostEstimate(
            flops=30 * len(EARLY) * CHUNK * xbc_width,
            bytes_accessed=6 * 1024 * 1024,
            transcendentals=len(EARLY) * CHUNK * xbc_width,
        ),
        name="early_chunks",
    )(*operands)


def inputs_kernel(heads, chunks, me_ref, *refs):
    arrays = refs[:ARRAYS]
    taps_ref, head_ref = refs[ARRAYS : ARRAYS + 2]
    xbc_ref, run_ref, col_ref, cum_ref, factor_ref, keep_ref = refs[ARRAYS + 2 : ARRAYS + 8]
    dt_ref = refs[ARRAYS + 8]
    width = heads * P_SIZE
    xbc_width = xbc_ref.shape[1]
    me = me_ref[0]
    for distance in range(chunks):
        j = lax.rem(me + distance, chunks)
        low = width + xbc_width
        dt_ref[j] = chunk_of(arrays, distance, low, low + heads).astype(jnp.float32)

    shifted = dt_ref[...] + head_ref[0]
    dt = jnp.maximum(shifted, 0.0) + jnp.log1p(jnp.exp(-jnp.abs(shifted)))
    run = (-head_ref[1] * dt).reshape(chunks * heads, CHUNK)
    lanes = lax.broadcasted_iota(jnp.int32, run.shape, 1)
    reach = 1
    while reach < CHUNK:
        run = run + jnp.where(lanes >= reach, pltpu.roll(run, reach, 1), 0.0)
        reach *= 2
    run = run.reshape(chunks, heads, CHUNK)
    total = jnp.broadcast_to(run[:, :, CHUNK - 1 :], run.shape)
    run_ref[...] = run
    col_ref[...] = run * LOG2E - jnp.log2(dt)
    factor_ref[...] = jnp.exp(total - run) * dt
    keep_ref[...] = jnp.exp(total)
    cum = jnp.zeros((heads, CHUNK), jnp.float32)
    for j in range(chunks):
        cum_ref[j] = cum
        cum = cum + total[j]
    cum_ref[chunks] = cum
    raws = {
        distance: chunk_of(arrays, distance, width, width + xbc_width)
        for distance in (LATE[0] - 1, *LATE)
    }
    convolve_chunks(raws, LATE, taps_ref, xbc_ref)


def chunk_inputs(me, arrays, taps, head_values):
    heads = head_values.shape[1]
    xbc_width = taps.shape[1]
    rows = sum(array.shape[1] for array in arrays)
    chunks = rows // CHUNK
    operands = [*arrays, taps, head_values]
    small = jax.ShapeDtypeStruct((chunks, heads, CHUNK), jnp.float32)
    results = [
        jax.ShapeDtypeStruct((len(LATE), xbc_width, CHUNK), jnp.bfloat16),
        small,
        small,
        jax.ShapeDtypeStruct((chunks + 1, heads, CHUNK), jnp.float32),
        small,
        small,
    ]
    return pl.pallas_call(
        functools.partial(inputs_kernel, heads, chunks),
        grid=(1,),
        in_specs=[pl.BlockSpec(memory_space=pltpu.SMEM)] + whole(*operands),
        out_specs=whole(*results),
        out_shape=results,
        scratch_shapes=[pltpu.VMEM((chunks, heads, CHUNK), jnp.float32)],
        compiler_params=pltpu.CompilerParams(vmem_limit_bytes=VMEM_LIMIT),
        cost_estimate=pl.CostEstimate(
            flops=30 * len(LATE) * CHUNK * xbc_width,
            bytes_accessed=6 * 1024 * 1024,
            transcendentals=len(LATE) * CHUNK * xbc_width,
        ),
        name="chunk_inputs",
    )(me, *operands)


def states_kernel(heads, chunks, me_ref, *refs):
    arrays = refs[:ARRAYS]
    halo_ref, early_ref, late_ref, taps_ref = refs[ARRAYS : ARRAYS + 4]
    cum_ref, factor_ref, keep_ref = refs[ARRAYS + 4 : ARRAYS + 7]
    xbc_ref, local_ref, payload_ref, raw_ref = refs[ARRAYS + 7 :]
    width = heads * P_SIZE
    xbc_width = xbc_ref.shape[1]
    for distance in range(chunks):

        @pl.when(lax.rem(me_ref[0] + distance, chunks) == 0)
        def _():
            raw_ref[...] = chunk_of(arrays, distance, width, width + xbc_width)

    for from_ref, distances in ((early_ref, EARLY), (late_ref, LATE)):
        for place, distance in enumerate(distances):
            xbc_ref[lax.rem(me_ref[0] + distance + chunks, chunks)] = from_ref[place]
    for at in range(0, xbc_width, P_SIZE):
        part = pl.ds(at, P_SIZE)
        xbc_ref[0, part, :] = convolve(
            raw_ref[part, :].astype(jnp.float32),
            halo_ref[part, :].astype(jnp.float32),
            taps_ref,
            at,
        )
    state = jnp.zeros((width, N), jnp.float32)
    for j in range(chunks):
        local_ref[j] = state
        added = added_state(xbc_ref[j], factor_ref[j], heads)
        state = state * rows_of_heads(keep_ref[j], heads) + added if j else added

    row = lax.broadcasted_iota(jnp.int32, (16, N), 0)
    all_keep = jnp.exp(cum_ref[chunks])
    high = all_keep.astype(jnp.bfloat16).astype(jnp.float32)
    mid = (all_keep - high).astype(jnp.bfloat16).astype(jnp.float32)
    low = all_keep - high - mid
    for piece in range(width // 16):
        h = piece * 16 // P_SIZE
        payload_ref[piece, :16, :] = state[piece * 16 : piece * 16 + 16].astype(jnp.bfloat16)
        parts = jnp.where(
            row == 0,
            jnp.broadcast_to(high[h : h + 1], (16, N)),
            jnp.where(
                row == 1,
                jnp.broadcast_to(mid[h : h + 1], (16, N)),
                jnp.broadcast_to(low[h : h + 1], (16, N)),
            ),
        )
        payload_ref[piece, 16:, :] = parts.astype(jnp.bfloat16)


def chunk_states(me, arrays, halo, early, late, taps, cum, factor, keep):
    heads = factor.shape[1]
    width = heads * P_SIZE
    xbc_width = taps.shape[1]
    chunks = factor.shape[0]
    operands = [*arrays, halo, early, late, taps, cum, factor, keep]
    results = [
        jax.ShapeDtypeStruct((chunks, xbc_width, CHUNK), jnp.bfloat16),
        jax.ShapeDtypeStruct((chunks, width, N), jnp.float32),
        jax.ShapeDtypeStruct((width // 16, 32, N), jnp.bfloat16),
    ]
    return pl.pallas_call(
        functools.partial(states_kernel, heads, chunks),
        grid=(1,),
        in_specs=[pl.BlockSpec(memory_space=pltpu.SMEM)] + whole(*operands),
        out_specs=whole(*results),
        out_shape=results,
        scratch_shapes=[pltpu.VMEM((xbc_width, CHUNK), jnp.bfloat16)],
        compiler_params=pltpu.CompilerParams(vmem_limit_bytes=VMEM_LIMIT),
        cost_estimate=pl.CostEstimate(
            flops=2 * chunks * CHUNK * width * N,
            bytes_accessed=8 * 1024 * 1024,
            transcendentals=CHUNK * xbc_width,
        ),
        name="chunk_states",
    )(me, *operands)


def prefix_kernel(got_ref, out_ref):
    count = got_ref.shape[0]
    tails = [got_ref[c, 16:, :].astype(jnp.float32) for c in range(count - 1)]
    keeps = [jnp.broadcast_to(tail[0:1] + tail[1:2] + tail[2:3], (16, N)) for tail in tails]
    state = jnp.zeros((16, N), jnp.float32)
    for c in range(count):
        out_ref[c] = state.astype(jnp.bfloat16)
        if c < count - 1:
            state = state * keeps[c] + got_ref[c, :16, :].astype(jnp.float32)


def prefix(got):
    count = got.shape[0]
    return pl.pallas_call(
        prefix_kernel,
        out_shape=jax.ShapeDtypeStruct((count, 16, N), jnp.bfloat16),
        compiler_params=pltpu.CompilerParams(vmem_limit_bytes=4 * 1024 * 1024),
        name="prefix",
    )(got)


def finish_kernel(heads, group, halves, me_ref, skip_ref, *refs):
    arrays = refs[:ARRAYS]
    xbc_ref, run_ref, col_ref, cum_ref, local_ref = refs[ARRAYS : ARRAYS + 5]
    state_ref, gain_ref, w_ref = refs[ARRAYS + 5 : ARRAYS + 8]
    outs = refs[ARRAYS + 8 : -2]
    hidden_ref, u_ref = refs[-2:]
    width = heads * P_SIZE
    count = len(PLACE_OF_DISTANCE)
    sender = lax.broadcasted_iota(jnp.int32, (CHUNK, CHUNK), 0)
    taker = lax.broadcasted_iota(jnp.int32, (CHUNK, CHUNK), 1)
    lower = sender <= taker
    before = state_ref[...].astype(jnp.float32)
    gains = jnp.transpose(gain_ref[...])
    gain = jnp.concatenate(
        [jnp.broadcast_to(gains[:, k : k + 1], (N, CHUNK)) for k in range(width // N)], axis=0
    )
    for place, distance in enumerate(group):
        j = lax.rem(me_ref[0] + distance + count, count)
        gates = chunk_of(arrays, distance % count, 0, width)
        b_t = xbc_ref[j, width : width + N, :]
        c_t = xbc_ref[j, width + N : width + 2 * N, :]
        scores = lax.dot_general(
            b_t, c_t, (((0,), (0,)), ((), ())), preferred_element_type=jnp.float32
        )
        run = run_ref[j]
        run2 = run * LOG2E
        columns = jnp.transpose(col_ref[j])
        start = local_ref[j] + before * rows_of_heads(jnp.exp(cum_ref[j]), heads)
        carried = jnp.dot(start.astype(jnp.bfloat16), c_t, preferred_element_type=jnp.float32)
        grown = jnp.exp(run)
        squares = jnp.zeros((P_SIZE, CHUNK), jnp.float32)
        for h in range(heads):
            part = slice(h * P_SIZE, (h + 1) * P_SIZE)
            spread = run2[h : h + 1, :] - columns[:, h : h + 1]
            weights = jnp.where(lower, scores * jnp.exp2(spread), 0.0).astype(jnp.bfloat16)
            x_t = xbc_ref[j, part, :]
            own = jnp.dot(x_t, weights, preferred_element_type=jnp.float32)
            y = own + carried[part, :] * grown[h : h + 1, :]
            gate = gates[part, :].astype(jnp.float32)
            opened = gate * (0.5 * jnp.tanh(0.5 * gate) + 0.5)
            u = (y + skip_ref[h] * x_t.astype(jnp.float32)) * opened
            squares = squares + u * u
            u_ref[part, :] = u
        mean = jnp.sum(squares, axis=0, keepdims=True) * (1.0 / width)
        hidden = u_ref[...] * lax.rsqrt(mean + 1e-05) * gain
        hidden_ref[place * CHUNK : (place + 1) * CHUNK, :] = jnp.transpose(
            hidden.astype(jnp.bfloat16)
        )
    w = w_ref[...]
    for at, (tall, out_ref) in enumerate(zip(halves, outs)):
        low = sum(halves[:at])
        out_ref[...] = jnp.dot(
            hidden_ref[low : low + tall, :], w, preferred_element_type=jnp.float32
        ).astype(jnp.bfloat16)


def finish(group, halves, me, skip, arrays, xbc, run, col, cum, local, state, gain, w_out):
    count = len(group)
    width, out_width = w_out.shape
    heads = width // P_SIZE
    operands = [*arrays, xbc, run, col, cum, local, state, gain, w_out]
    results = [jax.ShapeDtypeStruct((tall, out_width), jnp.bfloat16) for tall in halves]
    return pl.pallas_call(
        functools.partial(finish_kernel, heads, group, halves),
        grid=(1,),
        in_specs=[pl.BlockSpec(memory_space=pltpu.SMEM)] * 2 + whole(*operands),
        out_specs=whole(*results),
        out_shape=results,
        scratch_shapes=[
            pltpu.VMEM((count * CHUNK, width), jnp.bfloat16),
            pltpu.VMEM((width, CHUNK), jnp.float32),
        ],
        compiler_params=pltpu.CompilerParams(vmem_limit_bytes=VMEM_LIMIT),
        cost_estimate=pl.CostEstimate(
            flops=2 * count * CHUNK * width * (out_width + 2 * N),
            bytes_accessed=2 * width * out_width + count * 1024 * 1024,
            transcendentals=count * CHUNK * CHUNK * heads,
        ),
        name="finish",
    )(me, skip, *operands)


def add_kernel(*refs):
    total = refs[0][...].astype(jnp.float32)
    for ref in refs[1:-1]:
        total = total + ref[...].astype(jnp.float32)
    refs[-1][...] = total.astype(jnp.bfloat16)


def plus(moving, blocks, at):
    tall, wide = moving[0].shape
    return pl.pallas_call(
        add_kernel,
        grid=(1,),
        in_specs=[pl.BlockSpec((tall, wide), lambda i: (0, 0)) for _ in moving]
        + [pl.BlockSpec((tall, wide), lambda i: (at, 0))],
        out_specs=pl.BlockSpec((tall, wide), lambda i: (0, 0)),
        out_shape=jax.ShapeDtypeStruct((tall, wide), jnp.bfloat16),
        compiler_params=pltpu.CompilerParams(vmem_limit_bytes=8 * 1024 * 1024),
        cost_estimate=pl.CostEstimate(
            flops=tall * wide, bytes_accessed=6 * tall * wide, transcendentals=0
        ),
        name="plus",
    )(*moving, blocks)


def last_kernel(r0_ref, l0_ref, r1_ref, l1_ref, own_ref, out_ref):
    half = r0_ref.shape[0]
    for at, (right, left) in enumerate(((r0_ref, l0_ref), (r1_ref, l1_ref))):
        part = slice(at * half, (at + 1) * half)
        out_ref[part, :] = (
            right[...].astype(jnp.float32)
            + left[...].astype(jnp.float32)
            + own_ref[part, :].astype(jnp.float32)
        ).astype(jnp.bfloat16)


def last_sum(moving, blocks, at):
    tall, wide = moving[0].shape
    return pl.pallas_call(
        last_kernel,
        grid=(1,),
        in_specs=[pl.BlockSpec((tall, wide), lambda i: (0, 0)) for _ in moving]
        + [pl.BlockSpec((2 * tall, wide), lambda i: (at, 0))],
        out_specs=pl.BlockSpec((2 * tall, wide), lambda i: (0, 0)),
        out_shape=jax.ShapeDtypeStruct((2 * tall, wide), jnp.bfloat16),
        compiler_params=pltpu.CompilerParams(vmem_limit_bytes=8 * 1024 * 1024),
        name="last_sum",
    )(*moving, blocks)


def per_device(
    tokens, w_in, conv_weight, conv_bias, dt_bias, decay_rate, skip_scale, norm_gain, w_out
):
    me = lax.axis_index("tp")
    n_tp = lax.axis_size("tp")
    width = norm_gain.shape[0]
    heads = decay_rate.shape[0]
    rows = tokens.shape[0] * n_tp
    half = tokens.shape[0] // 2
    w_t = jnp.transpose(w_in.reshape(w_in.shape[0], w_in.shape[2]))
    xbc_width = conv_weight.shape[2]

    place = me.astype(jnp.int32).reshape(1)

    right, left = [None, None], [None, None]
    right[0], left[1], right[1], left[0] = halves(tokens)
    edges = {0: tokens[-8:]}
    arrays, pieces = [], []
    w_t = resident(w_t)
    for hop in range(1, 4):
        right[0] = turned(right[0], "tp", 1)
        left[1] = turned(left[1], "tp", -1)
        right[1] = turned(right[1], "tp", 1)
        left[0] = turned(left[0], "tp", -1)
        edges[hop], edges[n_tp - hop] = left[1][-8:], right[1][-8:]
        pieces += [right[0], left[1], right[1], left[0]]
        if hop < 3:
            if hop == 1:
                own = project([tokens], w_t)
            arrays.append(project(pieces, w_t))
            pieces = []
        if hop == 2:
            conv_weight, conv_bias, dt_bias, decay_rate, arrays[0] = lax.optimization_barrier(
                (conv_weight, conv_bias, dt_bias, decay_rate, arrays[0])
            )
            taps, head_values = along_lanes(
                conv_weight.reshape(conv_weight.shape[0], xbc_width),
                conv_bias,
                jnp.stack([dt_bias, decay_rate]),
            )
    last = [turned(right[0], "tp", 1), turned(left[1], "tp", -1)]
    arrays.append(project(pieces, w_t))

    edges[4] = last[1][-8:]
    edge = edges[0]
    for distance in range(1, n_tp):
        edge = jnp.where((me + distance) % n_tp == n_tp - 1, edges[distance], edge)
    edge = next_block(edge, 0)
    arrays += [own, project(last, w_t)]
    padding = jnp.zeros((CHUNK - edge.shape[0], edge.shape[1]), edge.dtype)
    halo = project([padding, edge], w_t[width : width + xbc_width])

    early = early_chunks(arrays[:-1], taps, width)
    late, run, col, cum, factor, keep = chunk_inputs(place, arrays, taps, head_values)
    xbc, local, payload = chunk_states(
        place, arrays, halo, early, late, taps, cum, factor, keep
    )
    got = lax.all_to_all(payload, "ctx", 0, 0, tiled=True)
    state = lax.all_to_all(prefix(got), "ctx", 0, 0, tiled=True).reshape(width, N)

    shared = (xbc, run, col, cum, local, state, norm_gain.reshape(width // N, N), w_out)
    blocks = {}
    for group in GROUPS:
        tall = (half, half) if group[0] == 4 else ()
        tall += (2 * half * (len(group) - len(tall) // 2),)
        made = finish(group, tall, place, skip_scale, arrays, *shared)
        for at, distance in enumerate(group):
            blocks[distance] = (made, at)

    def block(distance, part):
        made, at = blocks[distance]
        return made[-1], 2 * (at - len(made) // 2) + part

    r0, l1 = turned(blocks[4][0][0], "tp", 1), turned(blocks[4][0][1], "tp", -1)
    threes = blocks[3][0][-1]
    r1 = turned(threes[half : 2 * half], "tp", 1)
    l0 = turned(threes[2 * half : 3 * half], "tp", -1)
    for k in (3, 2, 1):
        r0 = turned(plus([r0], *block(k, 0)), "tp", 1)
        l1 = turned(plus([l1], *block(-k, 1)), "tp", -1)
        if k > 1:
            r1 = turned(plus([r1], *block(k - 1, 1)), "tp", 1)
            l0 = turned(plus([l0], *block(1 - k, 0)), "tp", -1)
    return last_sum([r0, l0, r1, l1], blocks[0][0][-1], blocks[0][1])


def solution(mesh):
    placed = (
        P(("ctx", "tp"), None),
        P(None, "tp", None),
        P(None, "tp", None),
        P("tp", None),
        P("tp"),
        P("tp"),
        P("tp"),
        P("tp"),
        P("tp", None),
    )
    return jax.shard_map(
        per_device, mesh=mesh, in_specs=placed, out_specs=P(("ctx", "tp"), None), check_vma=False
    )
```

```python
import functools
import math

import jax
import jax.numpy as jnp
from jax import lax
from jax.experimental import pallas as pl
from jax.experimental.pallas import tpu as pltpu
from jax.sharding import PartitionSpec as P

P_SIZE = 64
N = 128
CHUNK = 128
LOG2E = math.log2(math.e)
VMEM_LIMIT = 36 * 1024 * 1024

PLACE_OF_DISTANCE = ((3, 0), (0, 0), (1, 0), (2, 0), (4, 0), (2, 1), (1, 1), (0, 1))
ARRAYS = 5
HALVES = (0, 1, 1, 0)
EARLY = (-2, -1, 0, 1, 2, 3)
LATE = (4, 5)
GROUPS = ((4, 3, -3), (2, -2, 1, -1, 0))


def turned(value, axis, steps):
    count = lax.axis_size(axis)
    return lax.ppermute(value, axis, [(i, (i + steps) % count) for i in range(count)])


def next_block(value, steps):
    blocks, count = lax.axis_size("ctx"), lax.axis_size("tp")
    return lax.ppermute(
        value,
        ("ctx", "tp"),
        [
            (c * count + t, (c + 1) * count + (t + steps) % count)
            for c in range(blocks - 1)
            for t in range(count)
        ],
    )


def after(value, *earlier):
    return lax.optimization_barrier((value, *earlier))[0]


def rows_of_heads(per_head, heads):
    width = per_head.shape[1]
    return jnp.concatenate(
        [jnp.broadcast_to(per_head[h : h + 1], (P_SIZE, width)) for h in range(heads)], axis=0
    )


def project(pieces, w_t):
    rows = jnp.concatenate(pieces, axis=0) if len(pieces) > 1 else pieces[0]
    return lax.dot_general(
        w_t, rows, (((1,), (1,)), ((), ())), preferred_element_type=jnp.float32
    ).astype(jnp.bfloat16)


def resident_kernel(from_ref, to_ref):
    to_ref[...] = from_ref[...]


def resident(array):
    rows, columns = array.shape
    tile = 256
    return pl.pallas_call(
        resident_kernel,
        grid=(pl.cdiv(rows, tile),),
        in_specs=[pl.BlockSpec((tile, columns), lambda i: (i, 0))],
        out_specs=pl.BlockSpec((tile, columns), lambda i: (i, 0)),
        out_shape=jax.ShapeDtypeStruct(array.shape, array.dtype),
        compiler_params=pltpu.CompilerParams(vmem_limit_bytes=8 * 1024 * 1024),
        name="resident",
    )(array)


def halves_kernel(rows_ref, *out_refs):
    half = rows_ref.shape[0] // 2
    for out_ref, low in zip(out_refs, HALVES):
        out_ref[...] = rows_ref[low * half : (low + 1) * half, :]


def halves(rows):
    tall, wide = rows.shape
    result = jax.ShapeDtypeStruct((tall // 2, wide), rows.dtype)
    return pl.pallas_call(
        halves_kernel,
        grid=(1,),
        in_specs=whole(rows),
        out_specs=whole(*[result] * 4),
        out_shape=[result] * 4,
        compiler_params=pltpu.CompilerParams(vmem_limit_bytes=8 * 1024 * 1024),
        name="halves",
    )(rows)


def chunk_of(arrays, distance, low, high):
    which, side = PLACE_OF_DISTANCE[distance]
    rows = slice(low, high)
    if distance in (0, 4):
        return arrays[which][rows, side * CHUNK : (side + 1) * CHUNK]
    first = arrays[which][rows, :CHUNK].astype(jnp.float32)
    second = arrays[which][rows, CHUNK : 2 * CHUNK].astype(jnp.float32)
    second = pltpu.roll(second, CHUNK // 2, 1)
    upper = lax.broadcasted_iota(jnp.int32, first.shape, 1) < CHUNK // 2
    parts = (second, first) if side == 0 else (first, second)
    return jnp.where(upper, *parts).astype(jnp.bfloat16)


def whole(*shapes):
    def zeros(rank):
        return lambda i: (0,) * rank

    return [pl.BlockSpec(tuple(item.shape), zeros(len(item.shape))) for item in shapes]


def lanes_kernel(taps_ref, bias_ref, head_ref, wide_ref, wide_head_ref):
    count = taps_ref.shape[0]
    for at in range(0, taps_ref.shape[1], N):
        part = slice(at, at + N)
        columns = jnp.transpose(
            jnp.concatenate(
                [
                    taps_ref[:, part].astype(jnp.float32),
                    bias_ref[:, part].astype(jnp.float32),
                    jnp.zeros((7 - count, N), jnp.float32),
                ],
                axis=0,
            )
        )
        for k in range(count + 1):
            wide_ref[k, part, :] = jnp.broadcast_to(columns[:, k : k + 1], (N, CHUNK))
    heads = jnp.transpose(head_ref[...])
    for k in range(head_ref.shape[0]):
        wide_head_ref[k] = jnp.broadcast_to(heads[:, k : k + 1], wide_head_ref.shape[1:])


def along_lanes(taps, bias, head_values):
    results = [
        jax.ShapeDtypeStruct((taps.shape[0] + 1, taps.shape[1], CHUNK), jnp.float32),
        jax.ShapeDtypeStruct((*head_values.shape, CHUNK), jnp.float32),
    ]
    return pl.pallas_call(
        lanes_kernel,
        grid=(1,),
        in_specs=whole(taps, bias, head_values),
        out_specs=whole(*results),
        out_shape=results,
        compiler_params=pltpu.CompilerParams(vmem_limit_bytes=8 * 1024 * 1024),
        name="along_lanes",
    )(taps, bias, head_values)


def convolve(raw, before, taps_ref, at):
    part = pl.ds(at, P_SIZE)
    lanes = lax.broadcasted_iota(jnp.int32, raw.shape, 1)
    acc = taps_ref[4, part, :] + raw * taps_ref[3, part, :]
    for back in (1, 2, 3):
        moved = jnp.where(lanes < back, pltpu.roll(before, back, 1), pltpu.roll(raw, back, 1))
        acc = acc + moved * taps_ref[3 - back, part, :]
    return (acc * (0.5 * jnp.tanh(0.5 * acc) + 0.5)).astype(jnp.bfloat16)


def added_state(xbc, factor, heads):
    width = heads * P_SIZE
    inflow = (xbc[:width].astype(jnp.float32) * rows_of_heads(factor, heads)).astype(jnp.bfloat16)
    return lax.dot_general(
        inflow,
        xbc[width : width + N],
        (((1,), (1,)), ((), ())),
        preferred_element_type=jnp.float32,
    )


def convolve_chunks(raws, distances, taps_ref, xbc_ref):
    for place, distance in enumerate(distances):
        for at in range(0, xbc_ref.shape[1], P_SIZE):
            part = slice(at, at + P_SIZE)
            xbc_ref[place, part, :] = convolve(
                raws[distance][part].astype(jnp.float32),
                raws[distance - 1][part].astype(jnp.float32),
                taps_ref,
                at,
            )


def early_kernel(width, *refs):
    arrays, taps_ref, xbc_ref = refs[: ARRAYS - 1], refs[ARRAYS - 1], refs[ARRAYS]
    xbc_width = xbc_ref.shape[1]
    raws = {
        distance: chunk_of(arrays, distance % 8, width, width + xbc_width)
        for distance in (EARLY[0] - 1, *EARLY)
    }
    convolve_chunks(raws, EARLY, taps_ref, xbc_ref)


def early_chunks(arrays, taps, width):
    xbc_width = taps.shape[1]
    operands = [*arrays, taps]
    result = jax.ShapeDtypeStruct((len(EARLY), xbc_width, CHUNK), jnp.bfloat16)
    return pl.pallas_call(
        functools.partial(early_kernel, width),
        grid=(1,),
        in_specs=whole(*operands),
        out_specs=whole(result)[0],
        out_shape=result,
        compiler_params=pltpu.CompilerParams(vmem_limit_bytes=VMEM_LIMIT),
        cost_estimate=pl.CostEstimate(
            flops=30 * len(EARLY) * CHUNK * xbc_width,
            bytes_accessed=6 * 1024 * 1024,
            transcendentals=len(EARLY) * CHUNK * xbc_width,
        ),
        name="early_chunks",
    )(*operands)


def inputs_kernel(heads, chunks, me_ref, *refs):
    arrays = refs[:ARRAYS]
    taps_ref, head_ref = refs[ARRAYS : ARRAYS + 2]
    xbc_ref, run_ref, col_ref, cum_ref, factor_ref, keep_ref = refs[ARRAYS + 2 : ARRAYS + 8]
    dt_ref = refs[ARRAYS + 8]
    width = heads * P_SIZE
    xbc_width = xbc_ref.shape[1]
    me = me_ref[0]
    for distance in range(chunks):
        j = lax.rem(me + distance, chunks)
        low = width + xbc_width
        dt_ref[j] = chunk_of(arrays, distance, low, low + heads).astype(jnp.float32)

    shifted = dt_ref[...] + head_ref[0]
    dt = jnp.maximum(shifted, 0.0) + jnp.log1p(jnp.exp(-jnp.abs(shifted)))
    run = (-head_ref[1] * dt).reshape(chunks * heads, CHUNK)
    lanes = lax.broadcasted_iota(jnp.int32, run.shape, 1)
    reach = 1
    while reach < CHUNK:
        run = run + jnp.where(lanes >= reach, pltpu.roll(run, reach, 1), 0.0)
        reach *= 2
    run = run.reshape(chunks, heads, CHUNK)
    total = jnp.broadcast_to(run[:, :, CHUNK - 1 :], run.shape)
    run_ref[...] = run
    col_ref[...] = run * LOG2E - jnp.log2(dt)
    factor_ref[...] = jnp.exp(total - run) * dt
    keep_ref[...] = jnp.exp(total)
    cum = jnp.zeros((heads, CHUNK), jnp.float32)
    for j in range(chunks):
        cum_ref[j] = cum
        cum = cum + total[j]
    cum_ref[chunks] = cum
    raws = {
        distance: chunk_of(arrays, distance, width, width + xbc_width)
        for distance in (LATE[0] - 1, *LATE)
    }
    convolve_chunks(raws, LATE, taps_ref, xbc_ref)


def chunk_inputs(me, arrays, taps, head_values):
    heads = head_values.shape[1]
    xbc_width = taps.shape[1]
    rows = sum(array.shape[1] for array in arrays)
    chunks = rows // CHUNK
    operands = [*arrays, taps, head_values]
    small = jax.ShapeDtypeStruct((chunks, heads, CHUNK), jnp.float32)
    results = [
        jax.ShapeDtypeStruct((len(LATE), xbc_width, CHUNK), jnp.bfloat16),
        small,
        small,
        jax.ShapeDtypeStruct((chunks + 1, heads, CHUNK), jnp.float32),
        small,
        small,
    ]
    return pl.pallas_call(
        functools.partial(inputs_kernel, heads, chunks),
        grid=(1,),
        in_specs=[pl.BlockSpec(memory_space=pltpu.SMEM)] + whole(*operands),
        out_specs=whole(*results),
        out_shape=results,
        scratch_shapes=[pltpu.VMEM((chunks, heads, CHUNK), jnp.float32)],
        compiler_params=pltpu.CompilerParams(vmem_limit_bytes=VMEM_LIMIT),
        cost_estimate=pl.CostEstimate(
            flops=30 * len(LATE) * CHUNK * xbc_width,
            bytes_accessed=6 * 1024 * 1024,
            transcendentals=len(LATE) * CHUNK * xbc_width,
        ),
        name="chunk_inputs",
    )(me, *operands)


def states_kernel(heads, chunks, me_ref, *refs):
    arrays = refs[:ARRAYS]
    halo_ref, early_ref, late_ref, taps_ref = refs[ARRAYS : ARRAYS + 4]
    cum_ref, factor_ref, keep_ref = refs[ARRAYS + 4 : ARRAYS + 7]
    xbc_ref, local_ref, payload_ref, raw_ref = refs[ARRAYS + 7 :]
    width = heads * P_SIZE
    xbc_width = xbc_ref.shape[1]
    for distance in range(chunks):

        @pl.when(lax.rem(me_ref[0] + distance, chunks) == 0)
        def _():
            raw_ref[...] = chunk_of(arrays, distance, width, width + xbc_width)

    for from_ref, distances in ((early_ref, EARLY), (late_ref, LATE)):
        for place, distance in enumerate(distances):
            xbc_ref[lax.rem(me_ref[0] + distance + chunks, chunks)] = from_ref[place]
    for at in range(0, xbc_width, P_SIZE):
        part = pl.ds(at, P_SIZE)
        xbc_ref[0, part, :] = convolve(
            raw_ref[part, :].astype(jnp.float32),
            halo_ref[part, :].astype(jnp.float32),
            taps_ref,
            at,
        )
    state = jnp.zeros((width, N), jnp.float32)
    for j in range(chunks):
        local_ref[j] = state
        added = added_state(xbc_ref[j], factor_ref[j], heads)
        state = state * rows_of_heads(keep_ref[j], heads) + added if j else added

    row = lax.broadcasted_iota(jnp.int32, (16, N), 0)
    all_keep = jnp.exp(cum_ref[chunks])
    high = all_keep.astype(jnp.bfloat16).astype(jnp.float32)
    mid = (all_keep - high).astype(jnp.bfloat16).astype(jnp.float32)
    low = all_keep - high - mid
    for piece in range(width // 16):
        h = piece * 16 // P_SIZE
        payload_ref[piece, :16, :] = state[piece * 16 : piece * 16 + 16].astype(jnp.bfloat16)
        parts = jnp.where(
            row == 0,
            jnp.broadcast_to(high[h : h + 1], (16, N)),
            jnp.where(
                row == 1,
                jnp.broadcast_to(mid[h : h + 1], (16, N)),
                jnp.broadcast_to(low[h : h + 1], (16, N)),
            ),
        )
        payload_ref[piece, 16:, :] = parts.astype(jnp.bfloat16)


def chunk_states(me, arrays, halo, early, late, taps, cum, factor, keep):
    heads = factor.shape[1]
    width = heads * P_SIZE
    xbc_width = taps.shape[1]
    chunks = factor.shape[0]
    operands = [*arrays, halo, early, late, taps, cum, factor, keep]
    results = [
        jax.ShapeDtypeStruct((chunks, xbc_width, CHUNK), jnp.bfloat16),
        jax.ShapeDtypeStruct((chunks, width, N), jnp.float32),
        jax.ShapeDtypeStruct((width // 16, 32, N), jnp.bfloat16),
    ]
    return pl.pallas_call(
        functools.partial(states_kernel, heads, chunks),
        grid=(1,),
        in_specs=[pl.BlockSpec(memory_space=pltpu.SMEM)] + whole(*operands),
        out_specs=whole(*results),
        out_shape=results,
        scratch_shapes=[pltpu.VMEM((xbc_width, CHUNK), jnp.bfloat16)],
        compiler_params=pltpu.CompilerParams(vmem_limit_bytes=VMEM_LIMIT),
        cost_estimate=pl.CostEstimate(
            flops=2 * chunks * CHUNK * width * N,
            bytes_accessed=8 * 1024 * 1024,
            transcendentals=CHUNK * xbc_width,
        ),
        name="chunk_states",
    )(me, *operands)


def prefix_kernel(got_ref, out_ref):
    count = got_ref.shape[0]
    tails = [got_ref[c, 16:, :].astype(jnp.float32) for c in range(count - 1)]
    keeps = [jnp.broadcast_to(tail[0:1] + tail[1:2] + tail[2:3], (16, N)) for tail in tails]
    state = jnp.zeros((16, N), jnp.float32)
    for c in range(count):
        out_ref[c] = state.astype(jnp.bfloat16)
        if c < count - 1:
            state = state * keeps[c] + got_ref[c, :16, :].astype(jnp.float32)


def prefix(got):
    count = got.shape[0]
    return pl.pallas_call(
        prefix_kernel,
        out_shape=jax.ShapeDtypeStruct((count, 16, N), jnp.bfloat16),
        compiler_params=pltpu.CompilerParams(vmem_limit_bytes=4 * 1024 * 1024),
        name="prefix",
    )(got)


def finish_kernel(heads, group, halves, me_ref, skip_ref, *refs):
    arrays = refs[:ARRAYS]
    xbc_ref, run_ref, col_ref, cum_ref, local_ref = refs[ARRAYS : ARRAYS + 5]
    state_ref, gain_ref, w_ref = refs[ARRAYS + 5 : ARRAYS + 8]
    outs = refs[ARRAYS + 8 : -2]
    hidden_ref, u_ref = refs[-2:]
    width = heads * P_SIZE
    count = len(PLACE_OF_DISTANCE)
    sender = lax.broadcasted_iota(jnp.int32, (CHUNK, CHUNK), 0)
    taker = lax.broadcasted_iota(jnp.int32, (CHUNK, CHUNK), 1)
    lower = sender <= taker
    before = state_ref[...].astype(jnp.float32)
    gains = jnp.transpose(gain_ref[...])
    gain = jnp.concatenate(
        [jnp.broadcast_to(gains[:, k : k + 1], (N, CHUNK)) for k in range(width // N)], axis=0
    )
    for place, distance in enumerate(group):
        j = lax.rem(me_ref[0] + distance + count, count)
        gates = chunk_of(arrays, distance % count, 0, width)
        b_t = xbc_ref[j, width : width + N, :]
        c_t = xbc_ref[j, width + N : width + 2 * N, :]
        scores = lax.dot_general(
            b_t, c_t, (((0,), (0,)), ((), ())), preferred_element_type=jnp.float32
        )
        run = run_ref[j]
        run2 = run * LOG2E
        columns = jnp.transpose(col_ref[j])
        start = local_ref[j] + before * rows_of_heads(jnp.exp(cum_ref[j]), heads)
        carried = jnp.dot(start.astype(jnp.bfloat16), c_t, preferred_element_type=jnp.float32)
        grown = jnp.exp(run)
        squares = jnp.zeros((P_SIZE, CHUNK), jnp.float32)
        for h in range(heads):
            part = slice(h * P_SIZE, (h + 1) * P_SIZE)
            spread = run2[h : h + 1, :] - columns[:, h : h + 1]
            weights = jnp.where(lower, scores * jnp.exp2(spread), 0.0).astype(jnp.bfloat16)
            x_t = xbc_ref[j, part, :]
            own = jnp.dot(x_t, weights, preferred_element_type=jnp.float32)
            y = own + carried[part, :] * grown[h : h + 1, :]
            gate = gates[part, :].astype(jnp.float32)
            opened = gate * (0.5 * jnp.tanh(0.5 * gate) + 0.5)
            u = (y + skip_ref[h] * x_t.astype(jnp.float32)) * opened
            squares = squares + u * u
            u_ref[part, :] = u
        mean = jnp.sum(squares, axis=0, keepdims=True) * (1.0 / width)
        hidden = u_ref[...] * lax.rsqrt(mean + 1e-05) * gain
        hidden_ref[place * CHUNK : (place + 1) * CHUNK, :] = jnp.transpose(
            hidden.astype(jnp.bfloat16)
        )
    w = w_ref[...]
    for at, (tall, out_ref) in enumerate(zip(halves, outs)):
        low = sum(halves[:at])
        out_ref[...] = jnp.dot(
            hidden_ref[low : low + tall, :], w, preferred_element_type=jnp.float32
        ).astype(jnp.bfloat16)


def finish(group, halves, me, skip, arrays, xbc, run, col, cum, local, state, gain, w_out):
    count = len(group)
    width, out_width = w_out.shape
    heads = width // P_SIZE
    operands = [*arrays, xbc, run, col, cum, local, state, gain, w_out]
    results = [jax.ShapeDtypeStruct((tall, out_width), jnp.bfloat16) for tall in halves]
    return pl.pallas_call(
        functools.partial(finish_kernel, heads, group, halves),
        grid=(1,),
        in_specs=[pl.BlockSpec(memory_space=pltpu.SMEM)] * 2 + whole(*operands),
        out_specs=whole(*results),
        out_shape=results,
        scratch_shapes=[
            pltpu.VMEM((count * CHUNK, width), jnp.bfloat16),
            pltpu.VMEM((width, CHUNK), jnp.float32),
        ],
        compiler_params=pltpu.CompilerParams(vmem_limit_bytes=VMEM_LIMIT),
        cost_estimate=pl.CostEstimate(
            flops=2 * count * CHUNK * width * (out_width + 2 * N),
            bytes_accessed=2 * width * out_width + count * 1024 * 1024,
            transcendentals=count * CHUNK * CHUNK * heads,
        ),
        name="finish",
    )(me, skip, *operands)


def add_kernel(*refs):
    total = refs[0][...].astype(jnp.float32)
    for ref in refs[1:-1]:
        total = total + ref[...].astype(jnp.float32)
    refs[-1][...] = total.astype(jnp.bfloat16)


def plus(moving, blocks, at):
    tall, wide = moving[0].shape
    return pl.pallas_call(
        add_kernel,
        grid=(1,),
        in_specs=[pl.BlockSpec((tall, wide), lambda i: (0, 0)) for _ in moving]
        + [pl.BlockSpec((tall, wide), lambda i: (at, 0))],
        out_specs=pl.BlockSpec((tall, wide), lambda i: (0, 0)),
        out_shape=jax.ShapeDtypeStruct((tall, wide), jnp.bfloat16),
        compiler_params=pltpu.CompilerParams(vmem_limit_bytes=8 * 1024 * 1024),
        cost_estimate=pl.CostEstimate(
            flops=tall * wide, bytes_accessed=6 * tall * wide, transcendentals=0
        ),
        name="plus",
    )(*moving, blocks)


def last_kernel(r0_ref, l0_ref, r1_ref, l1_ref, own_ref, out_ref):
    half = r0_ref.shape[0]
    for at, (right, left) in enumerate(((r0_ref, l0_ref), (r1_ref, l1_ref))):
        part = slice(at * half, (at + 1) * half)
        out_ref[part, :] = (
            right[...].astype(jnp.float32)
            + left[...].astype(jnp.float32)
            + own_ref[part, :].astype(jnp.float32)
        ).astype(jnp.bfloat16)


def last_sum(moving, blocks, at):
    tall, wide = moving[0].shape
    return pl.pallas_call(
        last_kernel,
        grid=(1,),
        in_specs=[pl.BlockSpec((tall, wide), lambda i: (0, 0)) for _ in moving]
        + [pl.BlockSpec((2 * tall, wide), lambda i: (at, 0))],
        out_specs=pl.BlockSpec((2 * tall, wide), lambda i: (0, 0)),
        out_shape=jax.ShapeDtypeStruct((2 * tall, wide), jnp.bfloat16),
        compiler_params=pltpu.CompilerParams(vmem_limit_bytes=8 * 1024 * 1024),
        name="last_sum",
    )(*moving, blocks)


def per_device(
    tokens, w_in, conv_weight, conv_bias, dt_bias, decay_rate, skip_scale, norm_gain, w_out
):
    me = lax.axis_index("tp")
    n_tp = lax.axis_size("tp")
    width = norm_gain.shape[0]
    heads = decay_rate.shape[0]
    rows = tokens.shape[0] * n_tp
    half = tokens.shape[0] // 2
    w_t = jnp.transpose(w_in.reshape(w_in.shape[0], w_in.shape[2]))
    xbc_width = conv_weight.shape[2]

    place = me.astype(jnp.int32).reshape(1)

    right, left = [None, None], [None, None]
    right[0], left[1], right[1], left[0] = halves(tokens)
    edges = {0: tokens[-8:]}
    arrays, pieces = [], []
    w_t = resident(w_t)
    for hop in range(1, 4):
        right[0] = turned(right[0], "tp", 1)
        left[1] = turned(left[1], "tp", -1)
        right[1] = turned(right[1], "tp", 1)
        left[0] = turned(left[0], "tp", -1)
        edges[hop], edges[n_tp - hop] = left[1][-8:], right[1][-8:]
        pieces += [right[0], left[1], right[1], left[0]]
        if hop < 3:
            if hop == 1:
                own = project([tokens], w_t)
            arrays.append(project(pieces, w_t))
            pieces = []
        if hop == 2:
            conv_weight, conv_bias, dt_bias, decay_rate, arrays[0] = lax.optimization_barrier(
                (conv_weight, conv_bias, dt_bias, decay_rate, arrays[0])
            )
            taps, head_values = along_lanes(
                conv_weight.reshape(conv_weight.shape[0], xbc_width),
                conv_bias,
                jnp.stack([dt_bias, decay_rate]),
            )
    last = [turned(right[0], "tp", 1), turned(left[1], "tp", -1)]
    arrays.append(project(pieces, w_t))

    edges[4] = last[1][-8:]
    edge = edges[0]
    for distance in range(1, n_tp):
        edge = jnp.where((me + distance) % n_tp == n_tp - 1, edges[distance], edge)
    edge = next_block(edge, 0)
    arrays += [own, project(last, w_t)]
    padding = jnp.zeros((CHUNK - edge.shape[0], edge.shape[1]), edge.dtype)
    halo = project([padding, edge], w_t[width : width + xbc_width])

    early = early_chunks(arrays[:-1], taps, width)
    late, run, col, cum, factor, keep = chunk_inputs(place, arrays, taps, head_values)
    xbc, local, payload = chunk_states(
        place, arrays, halo, early, late, taps, cum, factor, keep
    )
    got = lax.all_to_all(payload, "ctx", 0, 0, tiled=True)
    state = lax.all_to_all(prefix(got), "ctx", 0, 0, tiled=True).reshape(width, N)

    shared = (xbc, run, col, cum, local, state, norm_gain.reshape(width // N, N), w_out)
    blocks = {}
    for group in GROUPS:
        tall = (half, half) if group[0] == 4 else ()
        tall += (2 * half * (len(group) - len(tall) // 2),)
        made = finish(group, tall, place, skip_scale, arrays, *shared)
        for at, distance in enumerate(group):
            blocks[distance] = (made, at)

    def block(distance, part):
        made, at = blocks[distance]
        return made[-1], 2 * (at - len(made) // 2) + part

    r0, l1 = turned(blocks[4][0][0], "tp", 1), turned(blocks[4][0][1], "tp", -1)
    threes = blocks[3][0][-1]
    r1 = turned(threes[half : 2 * half], "tp", 1)
    l0 = turned(threes[2 * half : 3 * half], "tp", -1)
    for k in (3, 2, 1):
        r0 = turned(plus([r0], *block(k, 0)), "tp", 1)
        l1 = turned(plus([l1], *block(-k, 1)), "tp", -1)
        if k > 1:
            r1 = turned(plus([r1], *block(k - 1, 1)), "tp", 1)
            l0 = turned(plus([l0], *block(1 - k, 0)), "tp", -1)
    return last_sum([r0, l0, r1, l1], blocks[0][0][-1], blocks[0][1])


def solution(mesh):
    placed = (
        P(("ctx", "tp"), None),
        P(None, "tp", None),
        P(None, "tp", None),
        P("tp", None),
        P("tp"),
        P("tp"),
        P("tp"),
        P("tp"),
        P("tp", None),
    )
    return jax.shard_map(
        per_device, mesh=mesh, in_specs=placed, out_specs=P(("ctx", "tp"), None), check_vma=False
    )
```
